128 devices in a mesh: layer: 4 (over z), tile: 32 (over x, y, core).
Axes of the slice: x: 4, y: 4, z: 4, core: 2. Of those that a mesh axis runs over, the one named last changes fastest.
Arguments:
- leaf_rhs: float32 [4, 128, 128, 256], P('layer', 'tile'), may hold values from -6 to 6
- leaf_inv: float32 [4, 128, 128, 128], P('layer', 'tile'), as said below
- par_rhs: float32 [4, 64, 128, 256], P('layer', 'tile'), may hold values from -6 to 6
- par_inv: float32 [4, 64, 128, 128], P('layer', 'tile'), as said below
- top_rhs: float32 [64, 128, 256], P('tile', None, 'layer'), may hold values from -6 to 6
- top_inv: float32 [64, 128, 128], P('tile'), as said below
- leaf_tiles: float32 [4, 5120, 128, 128], P('layer', 'tile'), may hold values from -0.125 to 0.125
- leaf_cols: int32 [4, 5120], P('layer', 'tile'), may hold values from 0 to 3
- leaf_rows: int32 [4, 5120], P('layer', 'tile'), may hold values from 0 to 127, as said below
- leaf_count: int32 [4, 32], P('layer', 'tile'), may hold values from 1 to 160, as said below
- par_tiles: float32 [4, 2560, 128, 128], P('layer', 'tile'), may hold values from -0.125 to 0.125
- par_cols: int32 [4, 2560], P('layer', 'tile'), may hold values from 0 to 1
- par_rows: int32 [4, 2560], P('layer', 'tile'), may hold values from 0 to 63
- par_count: int32 [4, 32], P('layer', 'tile'), may hold values from 1 to 80, as said below
Outputs:
- parent_solution: float32 [4, 64, 128, 256], P('layer', 'tile')
- top_solution: float32 [64, 128, 256], P('tile', None, 'layer')
The draws below stay inside these ranges and needn't reach their ends.
Inputs may be any that keep to these rules, and one draw needn't show every extreme that they name: `leaf_inv`: lower triangular, diagonal entries of magnitude 0.5 to 2. `par_inv`: lower triangular, diagonal entries of magnitude 0.5 to 2. `top_inv`: lower triangular, diagonal entries of magnitude 0.5 to 2. `leaf_rows`: the elimination subtree of a lower-level supernode of owner o lies in o's group of owners: owners o and q share a group when o // 2 % (4) equals q // 2 % 4; a tile below 64 names an upper-level supernode held by an owner of the same group, and the top-level supernodes are ancestors of every subtree. `leaf_count`: some owner of every layer has a full list. `par_count`: some owner of every layer has a full list.
All inputs are finite; a program needn't handle non-finite values.
Results may differ from the reference program's by a relative error of at most 0.0003.
Values sent between devices are 32-bit elements; how exact they have to be, the bound alone decides.
A program may use at most 128 MiB of HBM per device.

```python
import jax
import jax.numpy as jnp
from jax import lax

BS = 128
NRHS = 256
LEAF_DEV = 4
PAR_DEV = 2
LT_DEV = 160
PT_DEV = 80
LAYERS = 4
OWNERS = 32
LEAVES = 128
PARENTS = 64
TOP = 64
LT_ALL = 5120
PT_ALL = 2560


def lower_blocks(key, number):
    first, second, third = jax.random.split(key, 3)
    diagonal = jax.random.uniform(first, (number, BS), jnp.float32, 0.5, 2.0)
    spread = 0.6
    lower = jax.random.normal(second, (number, BS, BS), jnp.float32) * (spread / BS ** 0.5)
    lower = jnp.tril(lower, -1)
    sign = jnp.where(jax.random.bernoulli(third, 0.5, (number, BS)), 1.0, -1.0)
    eye = jnp.eye(BS, dtype=jnp.float32)
    return lower + eye[None] * (diagonal * sign)[:, :, None]


def list_counts(key, most):
    first, second = jax.random.split(key)
    shifts = jax.random.randint(first, (LAYERS, OWNERS), 0, 4)
    counts = jnp.maximum(jnp.right_shift(jnp.full((LAYERS, OWNERS), most, jnp.int32), shifts), 1)
    full_owner = jax.random.randint(second, (LAYERS, 1), 0, OWNERS)
    owner_index = jnp.arange(OWNERS, dtype=jnp.int32)[None, :]
    return jnp.where(owner_index == full_owner, most, counts).astype(jnp.int32)


def draw_leaf_inv(key, part):
    return lower_blocks(jax.random.fold_in(key, 11), LAYERS * LEAVES).reshape(LAYERS, LEAVES, BS, BS)


def draw_par_inv(key, part):
    return lower_blocks(jax.random.fold_in(key, 12), LAYERS * PARENTS).reshape(LAYERS, PARENTS, BS, BS)


def draw_top_inv(key, part):
    return lower_blocks(jax.random.fold_in(key, 13), TOP)


def draw_leaf_count(key, part):
    return list_counts(jax.random.fold_in(key, 21), LT_DEV)


def draw_par_count(key, part):
    return list_counts(jax.random.fold_in(key, 22), PT_DEV)


def draw_leaf_rows(key, part):
    first, second, third, fourth = jax.random.split(jax.random.fold_in(key, 31), 4)
    shape = (LAYERS, LT_ALL)
    owner = (jnp.arange(LT_ALL, dtype=jnp.int32) // LT_DEV)[None, :]
    groups = OWNERS // 8
    member = jax.random.randint(first, shape, 0, 8)
    target_owner = owner // 2 % groups * 2 + member % 2 + member // 2 * 2 * groups
    parent = target_owner * PAR_DEV + jax.random.randint(second, shape, 0, PAR_DEV)
    upper = PARENTS + jax.random.randint(third, shape, 0, TOP)
    picker = jax.random.randint(fourth, shape, 0, 2)
    return jnp.where(picker == 0, parent, upper).astype(jnp.int32)


def place_ends(drawn, rng, smallest, largest):
    spot = [jax.random.randint(jax.random.fold_in(rng, axis), (), 0, length) for axis, length in enumerate(drawn.shape)]
    widest = drawn.shape.index(max(drawn.shape))
    next_to = spot[:widest] + [(spot[widest] + 1) % drawn.shape[widest]] + spot[widest + 1:]
    return drawn.at[tuple(spot)].set(smallest).at[tuple(next_to)].set(largest)


def levels(own_key, shape, pieces, smallest, top_value):
    factor_of = 1.0
    for axis_at, blocks in pieces:
        draws = jax.random.uniform(jax.random.fold_in(jax.random.fold_in(own_key, 6), axis_at), (blocks,), jnp.float32, smallest / len(pieces), top_value / len(pieces))
        factor_of = factor_of * jnp.repeat(jnp.exp(draws), shape[axis_at] // blocks).reshape((-1,) + (1,) * (len(shape) - 1 - axis_at))
    return factor_of


def bell_draw(key, dims, width, limit, pieces=(), held_as=jnp.bfloat16):
    loudness = levels(key, dims, pieces, -0.22, 0.18) if pieces else 1.0
    values = jax.random.normal(key, dims, jnp.float32) * width * loudness
    return jnp.minimum(jnp.maximum(values, -limit), limit).astype(held_as)


def setup_inputs(seed: int = 0) -> dict:
    streams_of = jax.random.split(jax.random.key(seed), 15)
    leaf_rhs = bell_draw(streams_of[0], (LAYERS, LEAVES, BS, NRHS), 1.0, 6.0, ((0, 4), (1, 32)), jnp.float32)
    leaf_inv = draw_leaf_inv(jax.random.fold_in(streams_of[14], 71), 0)
    par_rhs = bell_draw(streams_of[2], (LAYERS, PARENTS, BS, NRHS), 1.0, 6.0, ((0, 4), (1, 32)), jnp.float32)
    par_inv = draw_par_inv(jax.random.fold_in(streams_of[14], 71), 0)
    top_rhs = bell_draw(streams_of[4], (TOP, BS, NRHS), 1.0, 6.0, ((0, 32), (2, 4)), jnp.float32)
    top_inv = draw_top_inv(jax.random.fold_in(streams_of[14], 71), 0)
    leaf_tiles = bell_draw(streams_of[6], (LAYERS, LT_ALL, BS, BS), (BS * 16) ** -0.5, 0.125, ((0, 4), (1, 32)), jnp.float32)
    leaf_cols = place_ends(jax.random.randint(streams_of[7], (LAYERS, LT_ALL), 0, LEAF_DEV), jax.random.fold_in(streams_of[7], 1), 0, LEAF_DEV - 1).astype(jnp.int32)
    leaf_rows = draw_leaf_rows(jax.random.fold_in(streams_of[14], 71), 0)
    leaf_count = draw_leaf_count(jax.random.fold_in(streams_of[14], 71), 0)
    par_tiles = bell_draw(streams_of[10], (LAYERS, PT_ALL, BS, BS), (BS * 16) ** -0.5, 0.125, ((0, 4), (1, 32)), jnp.float32)
    par_cols = place_ends(jax.random.randint(streams_of[11], (LAYERS, PT_ALL), 0, PAR_DEV), jax.random.fold_in(streams_of[11], 1), 0, PAR_DEV - 1).astype(jnp.int32)
    par_rows = place_ends(jax.random.randint(streams_of[12], (LAYERS, PT_ALL), 0, TOP), jax.random.fold_in(streams_of[12], 1), 0, TOP - 1).astype(jnp.int32)
    par_count = draw_par_count(jax.random.fold_in(streams_of[14], 71), 0)
    return {"leaf_rhs": leaf_rhs, "leaf_inv": leaf_inv, "par_rhs": par_rhs, "par_inv": par_inv, "top_rhs": top_rhs, "top_inv": top_inv, "leaf_tiles": leaf_tiles, "leaf_cols": leaf_cols, "leaf_rows": leaf_rows, "leaf_count": leaf_count, "par_tiles": par_tiles, "par_cols": par_cols, "par_rows": par_rows, "par_count": par_count}


def spread_update(tiles, cols, rows, count, solved, src_dev, per_dev, targets):
    highest = lax.Precision.HIGHEST
    tiles_owned = tiles.reshape(OWNERS, per_dev, BS, BS)
    cols_owned = cols.reshape(OWNERS, per_dev)
    rows_owned = rows.reshape(OWNERS, per_dev)

    def advance(total, item):
        tile_block, col_block, row_block, owner_count, owner = item
        source = owner * src_dev + col_block
        picked = jnp.take(solved, source.astype(jnp.int32), axis=0)
        product = jnp.einsum("tij,tjk->tik", tile_block, picked, precision=highest)
        in_use = jnp.arange(per_dev, dtype=jnp.int32) < owner_count
        product = jnp.where(in_use[:, None, None], product, jnp.zeros_like(product))
        return total + jax.ops.segment_sum(product, row_block, targets), None

    start = jnp.zeros((targets, BS, NRHS), jnp.float32)
    total, _ = lax.scan(advance, start, (tiles_owned, cols_owned, rows_owned, count, jnp.arange(OWNERS, dtype=jnp.int32)))
    return total


def reference(leaf_rhs, leaf_inv, par_rhs, par_inv, top_rhs, top_inv, leaf_tiles, leaf_cols, leaf_rows, leaf_count, par_tiles, par_cols, par_rows, par_count):
    highest = lax.Precision.HIGHEST
    ancestor = jnp.zeros((TOP, BS, NRHS), jnp.float32)
    parent_list = []
    for layer in range(LAYERS):
        leaf_solution = jnp.einsum("bij,bjk->bik", leaf_inv[layer], leaf_rhs[layer], precision=highest)
        leaf_update = spread_update(leaf_tiles[layer], leaf_cols[layer], leaf_rows[layer], leaf_count[layer], leaf_solution, LEAF_DEV, LT_DEV, PARENTS + TOP)
        parent_solution = jnp.einsum("bij,bjk->bik", par_inv[layer], par_rhs[layer] - leaf_update[:PARENTS], precision=highest)
        par_update = spread_update(par_tiles[layer], par_cols[layer], par_rows[layer], par_count[layer], parent_solution, PAR_DEV, PT_DEV, TOP)
        ancestor = ancestor + (leaf_update[PARENTS:] + par_update)
        parent_list.append(parent_solution)
    top_solution = jnp.einsum("bij,bjk->bik", top_inv, top_rhs - ancestor, precision=highest)
    return jnp.stack(parent_list), top_solution
```

```python
import jax
import jax.numpy as jnp
from jax import lax
from jax.experimental import pallas as pl
from jax.experimental.pallas import tpu as pltpu
from jax.sharding import PartitionSpec as P

MESH = pl.DeviceIdType.MESH
F32, BF16 = jnp.float32, jnp.bfloat16
BS, NR = 128, 256
CH = 16
UN = 4
ROWS = ((0, 48), (48, 40), (88, 40))
VMEM_LIMIT = 56 * 2**20


def split(t):
    hi = t.astype(BF16)
    return hi, (t - hi.astype(F32)).astype(BF16)


def lhs_cat(t):
    hi, lo = split(t)
    return jnp.concatenate([hi, lo, hi], axis=1)


def rhs_cat(t):
    hi, lo = split(t)
    return jnp.concatenate([hi, hi, lo], axis=0)


def local_kernel(
    lrow, lcol, lcnt, prow, pcol, pcnt, rhs, inv, ltiles, ptiles,
    g_out, l_out, v_out,
    xw, acc, vacc, lt, pt, lsem, psem, osem,
):
    nl, npar = lt.shape[0], pt.shape[0]
    count, pcount = lcnt[0, 0], pcnt[0, 0]

    def chunk(src, dst, sem, i):
        return pltpu.make_async_copy(src.at[pl.ds(i * CH, CH)], dst.at[pl.ds(i * CH, CH)], sem.at[i])

    for i in range(nl // CH):
        @pl.when(i * CH < count)
        def _():
            chunk(ltiles, lt, lsem, i).start()
    for i in range(npar // CH):
        @pl.when(i * CH < pcount)
        def _():
            chunk(ptiles, pt, psem, i).start()

    for c in range(4):
        x = jnp.dot(inv[c], rhs[c], precision=lax.Precision.HIGHEST, preferred_element_type=F32)
        xw[c] = rhs_cat(x)

    @pl.loop(0, acc.shape[0])
    def _(i):
        acc[i] = jnp.zeros((BS, NR), F32)

    @pl.loop(0, vacc.shape[0])
    def _(i):
        vacc[i] = jnp.zeros((2, BS, BS), F32)

    dummy = acc.shape[0] - 1

    def group(g, _):
        @pl.when(lax.rem(g, CH // UN) == 0)
        def _():
            chunk(ltiles, lt, lsem, g // (CH // UN)).wait()

        where, prods = [], []
        for u in range(UN):
            s = g * UN + u
            r = lrow[0, s]
            par = ((r >> 1) & 1) * 8 + (r >> 4) * 2 + (r & 1)
            t = r - 64
            top = 16 + ((t >> 1) & 1) * 32 + (t >> 2) * 2 + (t & 1)
            idx = jnp.where(r < 64, par, top)
            where.append(jnp.where(s < count, idx, dummy))
            prods.append(jnp.dot(lhs_cat(lt[s]), xw[lcol[0, s]], preferred_element_type=F32))
        for u in range(UN):
            acc[where[u]] += prods[u]
        return 0

    lax.fori_loop(0, (count + UN - 1) // UN, group, 0)
    g_copy = pltpu.make_async_copy(acc.at[pl.ds(0, 16)], g_out, osem.at[0])
    l_copy = pltpu.make_async_copy(acc.at[pl.ds(16, 64)], l_out, osem.at[1])
    g_copy.start()
    l_copy.start()

    def dense(s, _):
        @pl.when(lax.rem(s, CH) == 0)
        def _():
            chunk(ptiles, pt, psem, s // CH).wait()

        t = prow[0, s]
        top = ((t >> 1) & 1) * 32 + (t >> 2) * 2 + (t & 1)
        vacc[top, pcol[0, s]] += pt[s]
        return 0

    lax.fori_loop(0, pcount, dense, 0)
    v_copy = pltpu.make_async_copy(vacc, v_out, osem.at[2])
    v_copy.start()
    g_copy.wait()
    l_copy.wait()
    v_copy.wait()


def main_kernel(
    par_inv, par_rhs, top_inv, top_rhs, g, l, v,
    psol, tsol,
    g_own, g_sib, g_send, g_two, g_prev, g_next, x_own, x_sib, xw,
    l_own, l_sib, v_own, v_sib,
    d, e, f, h, two, prev, nxt, total,
    loc, sib_s, sib_r, gs, gr, rs_s, rs_r,
):
    z = lax.axis_index("layer")
    tile = lax.axis_index("tile")
    x, y, c = tile // 8, (tile // 2) % 4, tile % 2
    pos = (x, y, z)

    def at(axis, step):
        q = [x, y, z]
        q[axis] = (q[axis] + step + 4) % 4
        return (q[2], q[0] * 8 + q[1] * 2 + c)

    sib = (z, x * 8 + y * 2 + 1 - c)
    barrier = pltpu.get_barrier_semaphore()
    peers = [sib] + [at(a, s) for a in range(3) for s in (1, -1)]
    for p in peers:
        pl.semaphore_signal(barrier, inc=1, device_id=p, device_id_type=MESH)

    own = [
        pltpu.make_async_copy(g.at[c], g_own, loc.at[0]),
        pltpu.make_async_copy(v.at[c], v_own, loc.at[1]),
        pltpu.make_async_copy(l.at[c], l_own, loc.at[2]),
    ]
    for copy in own:
        copy.start()
    pl.semaphore_wait(barrier, len(peers))

    started = []

    def send(src, dst, ssem, rsem, device):
        copy = pltpu.make_async_remote_copy(
            src_ref=src, dst_ref=dst, send_sem=ssem, recv_sem=rsem, device_id=device, device_id_type=MESH
        )
        copy.start()
        started.append(copy)
        return copy

    order = [(x + 2) % 4, (x + 1) % 4, (x + 3) % 4, x]
    swap = [send(g.at[1 - c, q], g_sib.at[q], sib_s.at[i], sib_r.at[i], sib) for i, q in enumerate(order)]
    v_swap = send(v.at[1 - c], v_sib, sib_s.at[4], sib_r.at[4], sib)
    l_swap = send(l.at[1 - c], l_sib, sib_s.at[5], sib_r.at[5], sib)

    own[0].wait()
    right, left = at(0, 1), at(0, -1)
    for i in range(3):
        swap[i].wait_recv()
        g_send[i] = g_own[order[i]] + g_sib[order[i]]
        if i == 0:
            a2 = send(g_send.at[0, 0], g_two.at[0], gs.at[0], gr.at[0], right)
            b2 = send(g_send.at[0, 1], g_two.at[1], gs.at[1], gr.at[1], left)
        elif i == 1:
            p1 = send(g_send.at[1, 1], g_prev.at[1], gs.at[2], gr.at[2], right)
        else:
            n0 = send(g_send.at[2, 0], g_next.at[0], gs.at[3], gr.at[3], left)
    a2.wait_recv()
    g_send[1, 0] = g_send[1, 0] + g_two[0]
    p0 = send(g_send.at[1, 0], g_prev.at[0], gs.at[4], gr.at[4], right)
    b2.wait_recv()
    g_send[2, 1] = g_send[2, 1] + g_two[1]
    n1 = send(g_send.at[2, 1], g_next.at[1], gs.at[5], gr.at[5], left)
    swap[3].wait_recv()
    for copy in (p1, n0, p0, n1):
        copy.wait_recv()
    for j in range(2):
        update = g_own[x, j] + g_sib[x, j] + g_prev[j] + g_next[j]
        solved = jnp.dot(
            par_inv[j], par_rhs[j] - update, precision=lax.Precision.HIGHEST, preferred_element_type=F32
        )
        x_own[pl.ds(j * BS, BS)] = solved
        psol[j] = solved
    x_swap = send(x_own, x_sib, sib_s.at[6], sib_r.at[6], sib)
    xw[0] = rhs_cat(x_own[...])
    x_swap.wait_recv()
    xw[1] = rhs_cat(x_sib[...])
    own[1].wait()
    own[2].wait()
    v_swap.wait_recv()
    l_swap.wait_recv()

    low = lax.broadcasted_iota(jnp.int32, (BS, BS), 1) < 64

    @pl.loop(0, 16)
    def _(k):
        kx, ky = k // 4, k % 4
        sums = []
        for j in range(2):
            left_own = lhs_cat(jnp.concatenate([v_own[k, j, 0], v_own[k, j, 1]], axis=1))
            left_sib = lhs_cat(jnp.concatenate([v_sib[k, j, 0], v_sib[k, j, 1]], axis=1))
            sums.append(
                l_own[k, j] + l_sib[k, j]
                + jnp.dot(left_own, xw[0], preferred_element_type=F32)
                + jnp.dot(left_sib, xw[1], preferred_element_type=F32)
            )
        for half in range(2):
            first = sums[0][:, half * BS:(half + 1) * BS]
            second = pltpu.roll(sums[1][:, half * BS:(half + 1) * BS], 64, 1)
            for odd in range(2):
                q = jnp.where(low, second, first) if odd else jnp.where(low, first, second)
                kz = half * 2 + odd
                for p, spot in enumerate(((kx, ky, kz), (ky, kz, kx), (kz, kx, ky))):
                    d[p][spot[0], spot[1], spot[2]] = q[ROWS[p][0]:ROWS[p][0] + ROWS[p][1]]

    source = [d, e, f]
    target = [e, f, h]
    flying = {}

    def halves(p, ph):
        if ph < 2:
            return pl.ds(0, 2), pl.ds(2, 2)
        n = ROWS[p][1]
        a = (n // 16) * 8 + (8 if n % 16 else 0)
        return pl.ds(0, a), pl.ds(a, n - a)

    def issue(p, ph):
        axis = (p + ph) % 3
        m = pos[axis]
        src = source[ph][p]
        a, b = halves(p, ph)
        fwd, bwd = at(axis, 1), at(axis, -1)
        ss, rr = rs_s.at[p, ph], rs_r.at[p, ph]
        far, up, down = (m + 2) % 4, (m + 1) % 4, (m + 3) % 4
        flying[p, ph] = [
            send(src.at[far, a], two[ph][p].at[a], ss.at[0], rr.at[0], fwd),
            send(src.at[far, b], two[ph][p].at[b], ss.at[1], rr.at[1], bwd),
            send(src.at[up, b], prev[ph][p].at[b], ss.at[2], rr.at[2], fwd),
            send(src.at[down, a], nxt[ph][p].at[a], ss.at[3], rr.at[3], bwd),
        ]

    def middle(p, ph):
        axis = (p + ph) % 3
        m = pos[axis]
        src = source[ph][p]
        a, b = halves(p, ph)
        ss, rr = rs_s.at[p, ph], rs_r.at[p, ph]
        up, down = (m + 1) % 4, (m + 3) % 4
        copies = flying[p, ph]
        copies[0].wait_recv()
        src[up, a] = src[up, a] + two[ph][p][a]
        copies.append(send(src.at[up, a], prev[ph][p].at[a], ss.at[4], rr.at[4], at(axis, 1)))
        copies[1].wait_recv()
        src[down, b] = src[down, b] + two[ph][p][b]
        copies.append(send(src.at[down, b], nxt[ph][p].at[b], ss.at[5], rr.at[5], at(axis, -1)))

    def finish(p, ph):
        m = pos[(p + ph) % 3]
        for copy in flying[p, ph][2:]:
            copy.wait_recv()
        target[ph][p][...] = source[ph][p][m] + prev[ph][p][...] + nxt[ph][p][...]

    for p in range(3):
        issue(p, 0)
    for ph in range(3):
        for p in range(3):
            middle(p, ph)
        for p in range(3):
            finish(p, ph)
            if ph < 2:
                issue(p, ph + 1)

    for p in range(3):
        total[pl.ds(*ROWS[p])] = h[p][...]
    turned = pltpu.roll(total[...], 64, 1)
    odd = z % 2 == 1
    ancestor = (jnp.where(odd, turned, total[...]), jnp.where(odd, total[...], turned))
    for j in range(2):
        tsol[j] = jnp.dot(
            top_inv[j], top_rhs[j] - ancestor[j][:, :64], precision=lax.Precision.HIGHEST,
            preferred_element_type=F32,
        )
    for copy in started:
        copy.wait_send()


def local(
    leaf_rhs, leaf_inv, par_rhs, par_inv, top_rhs, top_inv, leaf_tiles, leaf_cols, leaf_rows, leaf_count,
    par_tiles, par_cols, par_rows, par_count,
):
    vm = pl.BlockSpec(memory_space=pltpu.VMEM)
    sm = pl.BlockSpec(memory_space=pltpu.SMEM)
    hb = pl.BlockSpec(memory_space=pl.ANY)
    nl, npar = leaf_tiles.shape[1], par_tiles.shape[1]
    shape = jax.ShapeDtypeStruct
    g, l, v = pl.pallas_call(
        local_kernel,
        out_shape=(
            shape((16, BS, NR), F32),
            shape((64, BS, NR), F32),
            shape((64, 2, BS, BS), F32),
        ),
        in_specs=[sm] * 6 + [vm, vm, hb, hb],
        out_specs=(hb, hb, hb),
        scratch_shapes=[
            pltpu.VMEM((4, 3 * BS, NR), BF16),
            pltpu.VMEM((81, BS, NR), F32),
            pltpu.VMEM((64, 2, BS, BS), F32),
            pltpu.VMEM((nl, BS, BS), F32),
            pltpu.VMEM((npar, BS, BS), F32),
            pltpu.SemaphoreType.DMA((nl // CH,)),
            pltpu.SemaphoreType.DMA((npar // CH,)),
            pltpu.SemaphoreType.DMA((3,)),
        ],
        compiler_params=pltpu.CompilerParams(vmem_limit_bytes=VMEM_LIMIT),
        name="leaf",
    )(leaf_rows, leaf_cols, leaf_count, par_rows, par_cols, par_count, leaf_rhs[0], leaf_inv[0], leaf_tiles[0], par_tiles[0])

    n = [r for _, r in ROWS]
    lead = ((4, 4), (4,), ())
    dma = pltpu.SemaphoreType.DMA

    def per_phase(extra):
        return [[pltpu.VMEM(extra + lead[ph] + (r, BS), F32) for r in n] for ph in range(3)]

    block = pltpu.VMEM((2, BS, NR), F32)
    psol, tsol = pl.pallas_call(
        main_kernel,
        out_shape=(shape((2, BS, NR), F32), shape((2, BS, 64), F32)),
        in_specs=[vm] * 4 + [hb] * 3,
        out_specs=(vm, vm),
        scratch_shapes=[
            pltpu.VMEM((4, 2, BS, NR), F32), pltpu.VMEM((4, 2, BS, NR), F32), pltpu.VMEM((3, 2, BS, NR), F32),
            block, block, block,
            pltpu.VMEM((2 * BS, NR), F32), pltpu.VMEM((2 * BS, NR), F32), pltpu.VMEM((2, 6 * BS, NR), BF16),
            pltpu.VMEM((16, 2, BS, NR), F32), pltpu.VMEM((16, 2, BS, NR), F32),
            pltpu.VMEM((16, 2, 2, BS, BS), F32), pltpu.VMEM((16, 2, 2, BS, BS), F32),
            [pltpu.VMEM((4, 4, 4, r, BS), F32) for r in n],
            [pltpu.VMEM((4, 4, r, BS), F32) for r in n],
            [pltpu.VMEM((4, r, BS), F32) for r in n],
            [pltpu.VMEM((r, BS), F32) for r in n],
            per_phase(()), per_phase(()), per_phase(()),
            pltpu.VMEM((BS, BS), F32),
            dma((3,)), dma((7,)), dma((7,)), dma((6,)), dma((6,)), dma((3, 3, 6)), dma((3, 3, 6)),
        ],
        compiler_params=pltpu.CompilerParams(
            collective_id=0, has_side_effects=True, vmem_limit_bytes=VMEM_LIMIT
        ),
        name="main",
    )(
        par_inv[0], par_rhs[0], top_inv, top_rhs,
        g.reshape(2, 4, 2, BS, NR), l.reshape(2, 16, 2, BS, NR), v.reshape(2, 16, 2, 2, BS, BS),
    )
    return psol[None], tsol


def solution(mesh):
    four = P("layer", "tile", None, None)
    pair = P("layer", "tile")
    top = P("tile", None, "layer")
    in_specs = (
        four, four, four, four, top, P("tile", None, None), four, pair, pair, pair, four, pair, pair, pair,
    )
    return jax.shard_map(local, mesh=mesh, in_specs=in_specs, out_specs=(four, top), check_vma=False)
```

```python
import jax
import jax.numpy as jnp
from jax import lax
from jax.experimental import pallas as pl
from jax.experimental.pallas import tpu as pltpu
from jax.sharding import PartitionSpec as P

MESH = pl.DeviceIdType.MESH
F32, BF16 = jnp.float32, jnp.bfloat16
BS, NR = 128, 256
CH = 16
UN = 16
ROWS = ((0, 48), (48, 48), (96, 32))
DIRECT = (1, 2)


def split(t):
    hi = t.astype(BF16)
    return hi, (t - hi.astype(F32)).astype(BF16)


def lhs_cat(t):
    hi, lo = split(t)
    return jnp.concatenate([hi, lo, hi], axis=1)


def rhs_cat(t):
    hi, lo = split(t)
    return jnp.concatenate([hi, hi, lo], axis=0)


def local_kernel(
    lrow, lcol, lcnt, prow, pcol, pcnt, rhs, inv, ltiles, ptiles,
    acc, vacc,
    xw, lt, pt, lsem, psem,
):
    nl, npar = lt.shape[0], pt.shape[0]
    count, pcount = lcnt[0, 0], pcnt[0, 0]

    def chunk(src, dst, sem, i):
        return pltpu.make_async_copy(src.at[pl.ds(i * CH, CH)], dst.at[pl.ds(i * CH, CH)], sem.at[i])

    for i in range(nl // CH):
        @pl.when(i * CH < count)
        def _():
            chunk(ltiles, lt, lsem, i).start()
    for i in range(npar // CH):
        @pl.when(i * CH < pcount)
        def _():
            chunk(ptiles, pt, psem, i).start()

    for c in range(4):
        x = jnp.dot(inv[c], rhs[c], precision=lax.Precision.HIGHEST, preferred_element_type=F32)
        xw[c] = rhs_cat(x)

    @pl.loop(0, acc.shape[0])
    def _(i):
        acc[i] = jnp.zeros((BS, NR), F32)

    @pl.loop(0, vacc.shape[0])
    def _(i):
        vacc[i] = jnp.zeros((2, BS, BS), F32)

    dummy = acc.shape[0] - 1

    def group(g, _):
        @pl.when(lax.rem(g, CH // UN) == 0)
        def _():
            chunk(ltiles, lt, lsem, g // (CH // UN)).wait()

        where, prods = [], []
        for u in range(UN):
            s = g * UN + u
            r = lrow[0, s]
            par = ((r >> 1) & 1) * 8 + (r >> 4) * 2 + (r & 1)
            t = r - 64
            top = 16 + ((t >> 1) & 1) * 32 + (t >> 2) * 2 + (t & 1)
            idx = jnp.where(r < 64, par, top)
            where.append(jnp.where(s < count, idx, dummy))
            prods.append(jnp.dot(lhs_cat(lt[s]), xw[lcol[0, s]], preferred_element_type=F32))
        for u in range(UN):
            acc[where[u]] += prods[u]
        return 0

    lax.fori_loop(0, (count + UN - 1) // UN, group, 0)
    def dense(s, _):
        @pl.when(lax.rem(s, CH) == 0)
        def _():
            chunk(ptiles, pt, psem, s // CH).wait()

        t = prow[0, s]
        top = ((t >> 1) & 1) * 32 + (t >> 2) * 2 + (t & 1)
        vacc[top, pcol[0, s]] += pt[s]
        return 0

    lax.fori_loop(0, pcount, dense, 0)


def main_kernel(
    par_inv, par_rhs, acc, v,
    x_own, total,
    g_sib, g_send, g_two, g_prev, g_next, x_sib, xw,
    l_sib, v_sib, vh, vl,
    d, e, f, h, two, prev, nxt,
    sib_s, sib_r, gs, gr, rs_s, rs_r,
):
    z = lax.axis_index("layer")
    tile = lax.axis_index("tile")
    x, y, c = tile // 8, (tile // 2) % 4, tile % 2
    pos = (x, y, z)

    def at(axis, step):
        q = [x, y, z]
        q[axis] = (q[axis] + step + 4) % 4
        return (q[2], q[0] * 8 + q[1] * 2 + c)

    sib = (z, x * 8 + y * 2 + 1 - c)
    barrier = pltpu.get_barrier_semaphore()
    peers = [sib] + [at(a, s) for a in range(3) for s in (1, -1, 2)]
    for p in peers:
        pl.semaphore_signal(barrier, inc=1, device_id=p, device_id_type=MESH)

    def split_v(src, base, side):
        @pl.loop(0, 16)
        def _(k):
            for j in range(2):
                for b in range(2):
                    hi, lo = split(src[base + k * 2 + j, b])
                    vh[side, k, j, :, b * BS:(b + 1) * BS] = hi
                    vl[side, k, j, :, b * BS:(b + 1) * BS] = lo

    split_v(v, c * 32, 0)
    pl.semaphore_wait(barrier, len(peers))

    started = []

    def send(src, dst, ssem, rsem, device):
        copy = pltpu.make_async_remote_copy(
            src_ref=src, dst_ref=dst, send_sem=ssem, recv_sem=rsem, device_id=device, device_id_type=MESH
        )
        copy.start()
        started.append(copy)
        return copy

    order = [(x + 2) % 4, (x + 1) % 4, (x + 3) % 4, x]
    yorder = [(y + 2) % 4, (y + 1) % 4, (y + 3) % 4, y]
    swap = [
        send(acc.at[pl.ds((1 - c) * 8 + q * 2, 2)], g_sib.at[q], sib_s.at[i], sib_r.at[i], sib)
        for i, q in enumerate(order)
    ]
    v_swap = send(v.at[pl.ds((1 - c) * 32, 32)], v_sib, sib_s.at[4], sib_r.at[4], sib)
    l_swap = [
        send(
            acc.at[pl.ds(16 + (1 - c) * 32 + q * 8, 8)], l_sib.at[pl.ds(q * 8, 8)],
            sib_s.at[5 + i], sib_r.at[5 + i], sib,
        )
        for i, q in enumerate(order)
    ]

    right, left = at(0, 1), at(0, -1)

    def both(q, j):
        return acc[c * 8 + q * 2 + j] + g_sib[q, j]

    for i in range(3):
        swap[i].wait_recv()
        for j in range(2):
            g_send[i, j] = both(order[i], j)
        if i == 0:
            a2 = send(g_send.at[0, 0], g_two.at[0], gs.at[0], gr.at[0], right)
            b2 = send(g_send.at[0, 1], g_two.at[1], gs.at[1], gr.at[1], left)
        elif i == 1:
            p1 = send(g_send.at[1, 1], g_prev.at[1], gs.at[2], gr.at[2], right)
        else:
            n0 = send(g_send.at[2, 0], g_next.at[0], gs.at[3], gr.at[3], left)
    a2.wait_recv()
    g_send[1, 0] = g_send[1, 0] + g_two[0]
    p0 = send(g_send.at[1, 0], g_prev.at[0], gs.at[4], gr.at[4], right)
    b2.wait_recv()
    g_send[2, 1] = g_send[2, 1] + g_two[1]
    n1 = send(g_send.at[2, 1], g_next.at[1], gs.at[5], gr.at[5], left)
    v_swap.wait_recv()
    split_v(v_sib, 0, 1)
    swap[3].wait_recv()
    for copy in (p1, n0, p0, n1):
        copy.wait_recv()
    for j in range(2):
        update = both(x, j) + g_prev[j] + g_next[j]
        x_own[j] = jnp.dot(
            par_inv[j], par_rhs[j] - update, precision=lax.Precision.HIGHEST, preferred_element_type=F32
        )
    x_swap = send(x_own, x_sib, sib_s.at[9], sib_r.at[9], sib)

    def set_weights(side, ref):
        for j in range(2):
            hi, lo = split(ref[j])
            xw[side, 0, pl.ds(j * BS, BS)] = hi
            xw[side, 1, pl.ds(j * BS, BS)] = lo

    set_weights(0, x_own)
    x_swap.wait_recv()
    set_weights(1, x_sib)

    low = lax.broadcasted_iota(jnp.int32, (BS, BS), 1) < 64

    def products(spots):
        for kx, ky in spots:
            k = kx * 4 + ky
            sums = []
            for j in range(2):
                part = acc[16 + c * 32 + k * 2 + j] + l_sib[k * 2 + j]
                for side in range(2):
                    hi, lo = vh[side, k, j], vl[side, k, j]
                    part = part + (
                        jnp.dot(hi, xw[side, 0], preferred_element_type=F32)
                        + jnp.dot(lo, xw[side, 0], preferred_element_type=F32)
                        + jnp.dot(hi, xw[side, 1], preferred_element_type=F32)
                    )
                sums.append(part)
            for half in range(2):
                first = sums[0][:, half * BS:(half + 1) * BS]
                second = pltpu.roll(sums[1][:, half * BS:(half + 1) * BS], 64, 1)
                for odd in range(2):
                    q = jnp.where(low, second, first) if odd else jnp.where(low, first, second)
                    kz = half * 2 + odd
                    for p, spot in enumerate(((kx, ky, kz), (ky, kz, kx), (kz, kx, ky))):
                        d[p][spot[0], spot[1], spot[2]] = q[ROWS[p][0]:ROWS[p][0] + ROWS[p][1]]

    source = [d, e, f]
    target = [e, f, h]
    first_half, second_half = pl.ds(0, 2), pl.ds(2, 2)
    flying = {(p, ph): [] for p in range(3) for ph in range(3)}

    def place(p, ph):
        axis = (p + ph) % 3
        m = pos[axis]
        return axis, m, source[ph][p], rs_s.at[p, ph], rs_r.at[p, ph]

    def far(p, ph):
        axis, m, src, ss, rr = place(p, ph)
        chunk = src.at[(m + 2) % 4]
        if ph in DIRECT:
            flying[p, ph].append(send(chunk, two[ph][p], ss.at[0], rr.at[0], at(axis, 2)))
        else:
            a, b = first_half, second_half
            flying[p, ph] += [
                send(chunk.at[a], two[ph][p].at[a], ss.at[0], rr.at[0], at(axis, 1)),
                send(chunk.at[b], two[ph][p].at[b], ss.at[1], rr.at[1], at(axis, -1)),
            ]

    def up(p, ph):
        axis, m, src, ss, rr = place(p, ph)
        chunk = src.at[(m + 1) % 4]
        b = second_half
        if ph in DIRECT:
            flying[p, ph].append(send(chunk, prev[ph][p], ss.at[2], rr.at[2], at(axis, 1)))
        else:
            flying[p, ph].append(send(chunk.at[b], prev[ph][p].at[b], ss.at[2], rr.at[2], at(axis, 1)))

    def down(p, ph):
        axis, m, src, ss, rr = place(p, ph)
        chunk = src.at[(m + 3) % 4]
        a = first_half
        if ph in DIRECT:
            flying[p, ph].append(send(chunk, nxt[ph][p], ss.at[3], rr.at[3], at(axis, -1)))
        else:
            flying[p, ph].append(send(chunk.at[a], nxt[ph][p].at[a], ss.at[3], rr.at[3], at(axis, -1)))

    def middle(p, ph):
        if ph in DIRECT:
            return
        axis, m, src, ss, rr = place(p, ph)
        a, b = first_half, second_half
        hi, lo = (m + 1) % 4, (m + 3) % 4
        copies = flying[p, ph]
        copies[0].wait_recv()
        src[hi, a] = src[hi, a] + two[ph][p][a]
        copies.append(send(src.at[hi, a], prev[ph][p].at[a], ss.at[4], rr.at[4], at(axis, 1)))
        copies[1].wait_recv()
        src[lo, b] = src[lo, b] + two[ph][p][b]
        copies.append(send(src.at[lo, b], nxt[ph][p].at[b], ss.at[5], rr.at[5], at(axis, -1)))

    def finish(p, ph):
        axis, m, src, ss, rr = place(p, ph)
        for copy in flying[p, ph] if ph in DIRECT else flying[p, ph][2:]:
            copy.wait_recv()
        got = src[m] + prev[ph][p][...] + nxt[ph][p][...]
        target[ph][p][...] = got + two[ph][p][...] if ph in DIRECT else got

    l_swap[0].wait_recv()
    products([(order[0], q) for q in yorder])
    far(0, 0)
    l_swap[1].wait_recv()
    l_swap[2].wait_recv()
    l_swap[3].wait_recv()
    products([(q, yorder[0]) for q in order[1:]])
    far(1, 0)
    products([(order[1], q) for q in yorder[1:]])
    up(0, 0)
    products([(q, yorder[1]) for q in order[2:]])
    up(1, 0)
    products([(order[2], q) for q in yorder[2:]])
    down(0, 0)
    products([(order[3], q) for q in yorder[2:]])
    down(1, 0)
    far(2, 0)
    up(2, 0)
    down(2, 0)
    for ph in range(3):
        for p in range(3):
            middle(p, ph)
        for p in range(3):
            finish(p, ph)
            if ph < 2:
                far(p, ph + 1)
                up(p, ph + 1)
                down(p, ph + 1)

    for p in range(3):
        total[pl.ds(*ROWS[p])] = h[p][...]
    total[...] = jnp.where(z % 2 == 1, pltpu.roll(total[...], 64, 1), total[...])
    for copy in started:
        copy.wait_send()


def tail_kernel(solved, total, inv, rhs, psol, tsol):
    psol[...] = solved[...]
    turned = total[...].T
    for j in range(2):
        tsol[j] = lax.dot_general(
            rhs[j] - turned[j * 64:(j + 1) * 64], inv[j], (((1,), (1,)), ((), ())),
            precision=lax.Precision.HIGHEST, preferred_element_type=F32,
        )


def leaf_call(*args):
    vm = pl.BlockSpec(memory_space=pltpu.VMEM)
    sm = pl.BlockSpec(memory_space=pltpu.SMEM)
    hb = pl.BlockSpec(memory_space=pl.ANY)
    nl, npar = args[8].shape[0], args[9].shape[0]
    shape = jax.ShapeDtypeStruct
    return pl.pallas_call(
        local_kernel,
        out_shape=(
            pltpu.VMEM((81, BS, NR), F32),
            pltpu.VMEM((64, 2, BS, BS), F32),
        ),
        in_specs=[sm] * 6 + [vm, vm, hb, hb],
        out_specs=(vm, vm),
        scratch_shapes=[
            pltpu.VMEM((4, 3 * BS, NR), BF16),
            pltpu.VMEM((nl, BS, BS), F32),
            pltpu.VMEM((npar, BS, BS), F32),
            pltpu.SemaphoreType.DMA((nl // CH,)),
            pltpu.SemaphoreType.DMA((npar // CH,)),
        ],
        compiler_params=pltpu.CompilerParams(vmem_limit_bytes=36*2**20),
        name="leaf",
    )(*args)


def local(
    leaf_rhs, leaf_inv, par_rhs, par_inv, top_rhs, top_inv, leaf_tiles, leaf_cols, leaf_rows, leaf_count,
    par_tiles, par_cols, par_rows, par_count,
):
    vm = pl.BlockSpec(memory_space=pltpu.VMEM)
    shape = jax.ShapeDtypeStruct
    acc, v = leaf_call(
        leaf_rows, leaf_cols, leaf_count, par_rows, par_cols, par_count,
        leaf_rhs[0], leaf_inv[0], leaf_tiles[0], par_tiles[0],
    )
    n = [r for _, r in ROWS]
    lead = ((4, 4), (4,), ())
    dma = pltpu.SemaphoreType.DMA

    def per_phase():
        return [[pltpu.VMEM(lead[ph] + (r, BS), F32) for r in n] for ph in range(3)]

    block = pltpu.VMEM((2, BS, NR), F32)
    solved, total = pl.pallas_call(
        main_kernel,
        out_shape=(pltpu.VMEM((2, BS, NR), F32), pltpu.VMEM((BS, BS), F32)),
        in_specs=[vm] * 4,
        out_specs=(vm, vm),
        scratch_shapes=[
            pltpu.VMEM((4, 2, BS, NR), F32), pltpu.VMEM((3, 2, BS, NR), F32), block, block, block,
            block, pltpu.VMEM((2, 2, 2 * BS, NR), BF16),
            pltpu.VMEM((32, BS, NR), F32), pltpu.VMEM((32, 2, BS, BS), F32),
            pltpu.VMEM((2, 16, 2, BS, NR), BF16), pltpu.VMEM((2, 16, 2, BS, NR), BF16),
            [pltpu.VMEM((4, 4, 4, r, BS), F32) for r in n],
            [pltpu.VMEM((4, 4, r, BS), F32) for r in n],
            [pltpu.VMEM((4, r, BS), F32) for r in n],
            [pltpu.VMEM((r, BS), F32) for r in n],
            per_phase(), per_phase(), per_phase(),
            dma((10,)), dma((10,)), dma((6,)), dma((6,)), dma((3, 3, 6)), dma((3, 3, 6)),
        ],
        compiler_params=pltpu.CompilerParams(
            collective_id=0, has_side_effects=True, vmem_limit_bytes=36 * 2**20
        ),
        name="main",
    )(
        par_inv[0], par_rhs[0],
        pltpu.with_memory_space_constraint(acc, pltpu.VMEM), pltpu.with_memory_space_constraint(v, pltpu.VMEM),
    )
    psol, tsol = pl.pallas_call(
        tail_kernel,
        out_shape=(shape((2, BS, NR), F32), shape((2, 64, BS), F32)),
        in_specs=[vm] * 4,
        out_specs=(vm, vm),
        name="tail",
    )(
        pltpu.with_memory_space_constraint(solved, pltpu.VMEM),
        pltpu.with_memory_space_constraint(total, pltpu.VMEM),
        top_inv, jnp.swapaxes(top_rhs, 1, 2),
    )
    return psol[None], jnp.swapaxes(tsol, 1, 2)


def solution(mesh):
    four = P("layer", "tile", None, None)
    pair = P("layer", "tile")
    top = P("tile", None, "layer")
    in_specs = (
        four, four, four, four, top, P("tile", None, None), four, pair, pair, pair, four, pair, pair, pair,
    )
    return jax.shard_map(local, mesh=mesh, in_specs=in_specs, out_specs=(four, top), check_vma=False)
```

```python
import jax
import jax.numpy as jnp
from jax import lax
from jax.experimental import pallas as pl
from jax.experimental.pallas import tpu as pltpu
from jax.sharding import PartitionSpec as P

MESH = pl.DeviceIdType.MESH
F32, BF16 = jnp.float32, jnp.bfloat16
BS, NR = 128, 256
CH = 16
UN = 16
PARTS = (
    ((0, 1, 2), 0, 48, 0),
    ((1, 0, 2), 48, 48, 0),
    ((2, 0, 1), 96, 16, None),
    ((0, 1, 2), 0, 48, 1),
    ((1, 0, 2), 48, 48, 1),
    ((2, 1, 0), 112, 16, None),
)
LAST = ((2, 0, 48), (2, 48, 48), (1, 96, 16), (0, 112, 16))
GOES = (0, 1, 2, 0, 1, 3)


def split(t):
    hi = t.astype(BF16)
    return hi, (t - hi.astype(F32)).astype(BF16)


def lhs_cat(t):
    hi, lo = split(t)
    return jnp.concatenate([hi, lo, hi], axis=1)


def rhs_cat(t):
    hi, lo = split(t)
    return jnp.concatenate([hi, hi, lo], axis=0)


def local_kernel(
    lrow, lcol, lcnt, prow, pcol, pcnt, rhs_in, inv_in, ltiles, ptiles,
    acc, vacc,
    xw, rhs, inv, lt, pt, lsem, psem, osem,
):
    nl, npar = lt.shape[0], pt.shape[0]
    count, pcount = lcnt[0, 0], pcnt[0, 0]

    def chunk(src, dst, sem, i):
        return pltpu.make_async_copy(src.at[pl.ds(i * CH, CH)], dst.at[pl.ds(i * CH, CH)], sem.at[i])

    first = (pltpu.make_async_copy(rhs_in, rhs, osem.at[0]), pltpu.make_async_copy(inv_in, inv, osem.at[1]))
    for copy in first:
        copy.start()
    for i in range(nl // CH):
        @pl.when(i * CH < count)
        def _():
            chunk(ltiles, lt, lsem, i).start()
    for i in range(npar // CH):
        @pl.when(i * CH < pcount)
        def _():
            chunk(ptiles, pt, psem, i).start()

    @pl.loop(0, acc.shape[0])
    def _(i):
        acc[i] = jnp.zeros((BS, NR), F32)

    @pl.loop(0, vacc.shape[0])
    def _(i):
        vacc[i] = jnp.zeros((2, BS, BS), F32)

    for copy in first:
        copy.wait()
    for c in range(4):
        x = jnp.dot(inv[c], rhs[c], precision=lax.Precision.HIGHEST, preferred_element_type=F32)
        xw[c] = rhs_cat(x)

    dummy = acc.shape[0] - 1

    def top_place(t):
        return ((t >> 1) & 1) * 32 + (t >> 2) * 2 + (t & 1)

    def group(g, _):
        @pl.when(lax.rem(g, CH // UN) == 0)
        def _():
            chunk(ltiles, lt, lsem, g // (CH // UN)).wait()

        where, prods = [], []
        for u in range(UN):
            s = g * UN + u
            r = lrow[0, s]
            par = ((r >> 1) & 1) * 8 + (r >> 4) * 2 + (r & 1)
            idx = jnp.where(r < 64, par, 16 + top_place(r - 64))
            where.append(jnp.where(s < count, idx, dummy))
            prods.append(jnp.dot(lhs_cat(lt[s]), xw[lcol[0, s]], preferred_element_type=F32))
        for u in range(UN):
            acc[where[u]] += prods[u]
        return 0

    lax.fori_loop(0, (count + UN - 1) // UN, group, 0)
    def dense(s, _):
        @pl.when(lax.rem(s, CH) == 0)
        def _():
            chunk(ptiles, pt, psem, s // CH).wait()

        vacc[top_place(prow[0, s]), pcol[0, s]] += pt[s]
        return 0

    lax.fori_loop(0, pcount, dense, 0)


def main_kernel(
    par_inv_in, par_rhs_in, top_inv_in, top_rhs_in, acc, v,
    x_own, tsol,
    par_inv, par_rhs, top_inv, top_rhs, total,
    g_sib, g_send, g_two, g_prev, g_next, x_sib, xw,
    l_sib, v_sib, vh, vl,
    d, e, f, two, prev, nxt,
    loc, v_sem, sib_s, sib_r, gs, gr, rs_s, rs_r, last_s, last_r,
):
    z = lax.axis_index("layer")
    tile = lax.axis_index("tile")
    x, y, c = tile // 8, (tile // 2) % 4, tile % 2
    pos = (x, y, z)

    def at(axis, step):
        q = [x, y, z]
        q[axis] = (q[axis] + step + 4) % 4
        return (q[2], q[0] * 8 + q[1] * 2 + c)

    sib = (z, x * 8 + y * 2 + 1 - c)
    barrier = pltpu.get_barrier_semaphore()
    peers = [sib] + [at(a, s) for a in range(3) for s in (1, -1, 2)]
    for p in peers:
        pl.semaphore_signal(barrier, inc=1, device_id=p, device_id_type=MESH)

    small = [
        pltpu.make_async_copy(src, dst, loc.at[i])
        for i, (src, dst) in enumerate(
            ((par_inv_in, par_inv), (par_rhs_in, par_rhs), (top_inv_in, top_inv), (top_rhs_in, top_rhs))
        )
    ]
    for copy in small:
        copy.start()

    def split_v(src, base, side):
        @pl.loop(0, 16)
        def _(k):
            for j in range(2):
                for b in range(2):
                    hi, lo = split(src[base + k * 2 + j, b])
                    vh[side, k, j, :, b * BS:(b + 1) * BS] = hi
                    vl[side, k, j, :, b * BS:(b + 1) * BS] = lo

    split_v(v, c * 32, 0)
    pl.semaphore_wait(barrier, len(peers))

    started = []

    def send(src, dst, ssem, rsem, device):
        copy = pltpu.make_async_remote_copy(
            src_ref=src, dst_ref=dst, send_sem=ssem, recv_sem=rsem, device_id=device, device_id_type=MESH
        )
        copy.start()
        started.append(copy)
        return copy

    def leave(*copies):
        for copy in copies:
            copy.wait_send()
            started[:] = [other for other in started if other is not copy]

    order = [(x + 2) % 4, (x + 1) % 4, (x + 3) % 4, x]
    yorder = [(y + 2) % 4, (y + 1) % 4, (y + 3) % 4, y]
    col = (pl.ds(0, BS), pl.ds(BS, BS))

    def swap_g(i, half):
        q = order[i]
        return send(
            acc.at[pl.ds((1 - c) * 8 + q * 2, 2), :, col[half]], g_sib.at[q, :, :, col[half]],
            sib_s.at[half, i], sib_r.at[half, i], sib,
        )

    def swap_l(i, half):
        q = order[i]
        return send(
            acc.at[pl.ds(16 + (1 - c) * 32 + q * 8, 8), :, col[half]], l_sib.at[pl.ds(q * 8, 8), :, col[half]],
            sib_s.at[half, 4 + i], sib_r.at[half, 4 + i], sib,
        )

    right, left = at(0, 1), at(0, -1)
    ring = [{}, {}]

    def gather(i, half):
        swap[half][i].wait_recv()
        q, cut = order[i], col[half]
        for j in range(2):
            g_send[i, j, :, cut] = acc[c * 8 + q * 2 + j, :, cut] + g_sib[q, j, :, cut]

    def hop(half, name, i, src, dst, device):
        cut = col[half]
        ring[half][name] = send(src.at[:, cut], dst.at[:, cut], gs.at[half, i], gr.at[half, i], device)

    def far_g(half):
        hop(half, "a2", 0, g_send.at[0, 0], g_two.at[0], right)
        hop(half, "b2", 1, g_send.at[0, 1], g_two.at[1], left)

    def near_g(half):
        hop(half, "p1", 2, g_send.at[1, 1], g_prev.at[1], right)
        hop(half, "n0", 3, g_send.at[2, 0], g_next.at[0], left)

    def relay_g(half):
        cut = col[half]
        ring[half]["a2"].wait_recv()
        g_send[1, 0, :, cut] = g_send[1, 0, :, cut] + g_two[0, :, cut]
        hop(half, "p0", 4, g_send.at[1, 0], g_prev.at[0], right)
        ring[half]["b2"].wait_recv()
        g_send[2, 1, :, cut] = g_send[2, 1, :, cut] + g_two[1, :, cut]
        hop(half, "n1", 5, g_send.at[2, 1], g_next.at[1], left)

    def solve(half):
        cut = col[half]
        for name in ("p1", "n0", "p0", "n1"):
            ring[half][name].wait_recv()
        for j in range(2):
            known = acc[c * 8 + x * 2 + j, :, cut] + g_sib[x, j, :, cut] + g_prev[j, :, cut] + g_next[j, :, cut]
            x_own[j, :, cut] = jnp.dot(
                par_inv[j], par_rhs[j, :, cut] - known, precision=lax.Precision.HIGHEST, preferred_element_type=F32
            )
        return send(
            x_own.at[:, :, col[half]], x_sib.at[:, :, col[half]], sib_s.at[half, 8], sib_r.at[half, 8], sib
        )

    def set_weights(half, side, ref):
        for j in range(2):
            hi, lo = split(ref[j, :, col[half]])
            xw[half, side, pl.ds(j * BS, BS), col[0]] = hi
            xw[half, side, pl.ds(j * BS, BS), col[1]] = lo

    swap = [[swap_g(0, 0)], []]
    leave(swap[0][0])
    swap[1].append(swap_g(0, 1))
    swap[0] += [swap_g(1, 0), swap_g(2, 0)]
    swap[1] += [swap_g(1, 1), swap_g(2, 1)]
    swap[0].append(swap_g(3, 0))
    swap[1].append(swap_g(3, 1))
    gather(0, 0)
    far_g(0)
    gather(0, 1)
    far_g(1)
    leave(*swap[0][1:3], *swap[1][:3])
    v_swap = send(v.at[pl.ds((1 - c) * 32, 32)], v_sib, v_sem.at[0], v_sem.at[1], sib)
    for half in range(2):
        gather(1, half)
        gather(2, half)
    leave(ring[0]["a2"], ring[0]["b2"])
    near_g(0)
    relay_g(0)
    leave(ring[0]["p0"], ring[0]["n1"])
    near_g(1)
    relay_g(1)
    leave(v_swap)
    l_swap = [[swap_l(i, 0) for i in range(4)], []]
    v_swap.wait_recv()
    split_v(v_sib, 0, 1)
    small[0].wait()
    small[1].wait()
    for half in range(2):
        swap[half][3].wait_recv()
    x_swap = [solve(0)]
    set_weights(0, 0, x_own)
    l_swap[1] += [swap_l(0, 1), swap_l(1, 1)]
    x_swap[0].wait_recv()
    set_weights(0, 1, x_sib)

    low = lax.broadcasted_iota(jnp.int32, (BS, BS), 1) < 64

    def products(half, spots):
        for kx, ky in spots:
            k = kx * 4 + ky
            main, fine = jnp.zeros((2 * BS, NR), F32), jnp.zeros((2 * BS, BS), F32)
            for side in range(2):
                weights = xw[half, side]
                main = main + jnp.dot(
                    vh[side, k].reshape(2 * BS, NR), weights, preferred_element_type=F32
                )
                fine = fine + jnp.dot(
                    vl[side, k].reshape(2 * BS, NR), weights[:, :BS], preferred_element_type=F32
                )
            both = main[:, :BS] + (main[:, BS:] + fine)
            sums = [
                both[j * BS:(j + 1) * BS]
                + (acc[16 + c * 32 + k * 2 + j, :, col[half]] + l_sib[k * 2 + j, :, col[half]])
                for j in range(2)
            ]
            second = pltpu.roll(sums[1], 64, 1)
            for odd in range(2):
                q = jnp.where(low, second, sums[0]) if odd else jnp.where(low, sums[0], second)
                for p, (axes, row, n, of) in enumerate(PARTS):
                    if of not in (None, half):
                        continue
                    spot = (kx, ky, odd if of is not None else half * 2 + odd)
                    s0, s1, s2 = (spot[axis] for axis in axes)
                    d[p][s0, s1, s2] = q[row:row + n]

    front, back = pl.ds(0, 2), pl.ds(2, 2)
    flying = {}

    def place(p):
        axis = PARTS[p][0][0]
        return axis, pos[axis], d[p], rs_s.at[p, 0], rs_r.at[p, 0]

    def far(p):
        axis, m, src, ss, rr = place(p)
        chunk, there = src.at[(m + 2) % 4], two[0][p]
        flying[p, "far"] = [
            send(chunk.at[front], there.at[front], ss.at[0], rr.at[0], at(axis, 1)),
            send(chunk.at[back], there.at[back], ss.at[1], rr.at[1], at(axis, -1)),
        ]

    def near(p):
        axis, m, src, ss, rr = place(p)
        flying[p, "near"] = [
            send(src.at[(m + 1) % 4, back], prev[0][p].at[back], ss.at[2], rr.at[2], at(axis, 1)),
            send(src.at[(m + 3) % 4, front], nxt[0][p].at[front], ss.at[3], rr.at[3], at(axis, -1)),
        ]

    def relay(p):
        axis, m, src, ss, rr = place(p)
        hi, lo = (m + 1) % 4, (m + 3) % 4
        ahead, behind = flying[p, "far"]
        ahead.wait_recv()
        src[hi, front] = src[hi, front] + two[0][p][front]
        one = send(src.at[hi, front], prev[0][p].at[front], ss.at[4], rr.at[4], at(axis, 1))
        behind.wait_recv()
        src[lo, back] = src[lo, back] + two[0][p][back]
        other = send(src.at[lo, back], nxt[0][p].at[back], ss.at[5], rr.at[5], at(axis, -1))
        flying[p, "relay"] = [one, other]

    def straight(key, axis, src, ph, i, ss, rr):
        m = pos[axis]
        flying[key] = [
            send(src.at[(m + step) % 4], there[ph][i], ss.at[k], rr.at[k], at(axis, step))
            for k, (step, there) in enumerate(((2, two), (1, prev), (3, nxt)))
        ]

    def received(key, axis, src, ph, i):
        for copy in flying[key]:
            copy.wait_recv()
        return src[pos[axis]] + prev[ph][i][...] + nxt[ph][i][...] + two[ph][i][...]

    def second_phase(p):
        axis, m, src, ss, rr = place(p)
        for copy in flying[p, "near"] + flying[p, "relay"]:
            copy.wait_recv()
        e[p][...] = src[m] + prev[0][p][...] + nxt[0][p][...]
        straight((p, 1), PARTS[p][0][1], e[p], 1, p, rs_s.at[p, 1], rs_r.at[p, 1])

    def join(p):
        got = received((p, 1), PARTS[p][0][1], e[p], 1, p)
        of = PARTS[p][3]
        if of is None:
            f[GOES[p]][...] = got
        else:
            f[GOES[p]][pl.ds(2 * of, 2)] = got

    def third_phase(i):
        straight((i, 2), LAST[i][0], f[i], 2, i, last_s.at[i], last_r.at[i])

    l_swap[0][0].wait_recv()
    products(0, [(order[0], q) for q in yorder])
    far(0)
    for i in (1, 2, 3):
        l_swap[0][i].wait_recv()
    products(0, [(q, yorder[0]) for q in order[1:]])
    far(1)
    x_swap.append(solve(1))
    l_swap[1] += [swap_l(2, 1), swap_l(3, 1)]
    products(0, [(q, k) for q in order[1:] for k in yorder[1:]])
    near(0)
    near(1)
    set_weights(1, 0, x_own)
    x_swap[1].wait_recv()
    set_weights(1, 1, x_sib)
    l_swap[1][0].wait_recv()
    products(1, [(order[0], q) for q in yorder])
    far(3)
    for i in (1, 2, 3):
        l_swap[1][i].wait_recv()
    products(1, [(q, yorder[0]) for q in order[1:]])
    far(4)
    relay(0)
    relay(1)
    products(1, [(q, k) for q in order[1:] for k in yorder[1:]])
    far(2)
    far(5)
    near(3)
    near(4)
    near(2)
    relay(3)
    relay(4)
    relay(2)
    near(5)
    second_phase(0)
    second_phase(1)
    relay(5)
    for p in (3, 4, 2, 5):
        second_phase(p)
    join(0)
    join(1)
    join(3)
    third_phase(0)
    join(4)
    third_phase(1)
    join(2)
    third_phase(2)
    join(5)
    third_phase(3)
    for i, (axis, row, n) in enumerate(LAST):
        total[pl.ds(row, n)] = received((i, 2), axis, f[i], 2, i)

    turned = jnp.where(z % 2 == 1, pltpu.roll(total[...], 64, 1), total[...]).T
    small[2].wait()
    small[3].wait()
    for j in range(2):
        tsol[j] = lax.dot_general(
            top_rhs[j] - turned[j * 64:(j + 1) * 64], top_inv[j], (((1,), (1,)), ((), ())),
            precision=lax.Precision.HIGHEST, preferred_element_type=F32,
        )
    for copy in started:
        copy.wait_send()


def tail_kernel(solved, top, psol, tsol, sem):
    copies = (pltpu.make_async_copy(solved, psol, sem.at[0]), pltpu.make_async_copy(top, tsol, sem.at[1]))
    for copy in copies:
        copy.start()
    for copy in copies:
        copy.wait()


def leaf_call(*args):
    vm = pl.BlockSpec(memory_space=pltpu.VMEM)
    sm = pl.BlockSpec(memory_space=pltpu.SMEM)
    hb = pl.BlockSpec(memory_space=pl.ANY)
    nl, npar = args[8].shape[0], args[9].shape[0]
    shape = jax.ShapeDtypeStruct
    return pl.pallas_call(
        local_kernel,
        out_shape=(
            pltpu.VMEM((81, BS, NR), F32),
            pltpu.VMEM((64, 2, BS, BS), F32),
        ),
        in_specs=[sm] * 6 + [hb] * 4,
        out_specs=(vm, vm),
        scratch_shapes=[
            pltpu.VMEM((4, 3 * BS, NR), BF16),
            pltpu.VMEM((4, BS, NR), F32),
            pltpu.VMEM((4, BS, BS), F32),
            pltpu.VMEM((nl, BS, BS), F32),
            pltpu.VMEM((npar, BS, BS), F32),
            pltpu.SemaphoreType.DMA((nl // CH,)),
            pltpu.SemaphoreType.DMA((npar // CH,)),
            pltpu.SemaphoreType.DMA((2,)),
        ],
        compiler_params=pltpu.CompilerParams(vmem_limit_bytes=36*2**20),
        name="leaf",
    )(*args)


def local(
    leaf_rhs, leaf_inv, par_rhs, par_inv, top_rhs, top_inv, leaf_tiles, leaf_cols, leaf_rows, leaf_count,
    par_tiles, par_cols, par_rows, par_count,
):
    vm = pl.BlockSpec(memory_space=pltpu.VMEM)
    shape = jax.ShapeDtypeStruct
    acc, v = leaf_call(
        leaf_rows, leaf_cols, leaf_count, par_rows, par_cols, par_count,
        leaf_rhs[0], leaf_inv[0], leaf_tiles[0], par_tiles[0],
    )
    dma = pltpu.SemaphoreType.DMA
    hb = pl.BlockSpec(memory_space=pl.ANY)
    whole = [(4, 4, 4 if of is None else 2, n, BS) for _, _, n, of in PARTS]
    joined = [(4, n, BS) for _, _, n in LAST]
    phases = [[q[1:] for q in whole], [q[2:] for q in whole], [q[1:] for q in joined]]

    def vmem(shapes):
        return [pltpu.VMEM(q, F32) for q in shapes]

    block, square, slim = pltpu.VMEM((2, BS, NR), F32), pltpu.VMEM((2, BS, BS), F32), pltpu.VMEM((2, 64, BS), F32)
    solved, top = pl.pallas_call(
        main_kernel,
        out_shape=(block, slim),
        in_specs=[hb] * 4 + [vm] * 2,
        out_specs=(vm, vm),
        scratch_shapes=[
            square, block, square, slim, pltpu.VMEM((BS, BS), F32),
            pltpu.VMEM((4, 2, BS, NR), F32), pltpu.VMEM((3, 2, BS, NR), F32), block, block, block,
            block, pltpu.VMEM((2, 2, 2 * BS, 2 * BS), BF16),
            pltpu.VMEM((32, BS, NR), F32), pltpu.VMEM((32, 2, BS, BS), F32),
            pltpu.VMEM((2, 16, 2, BS, NR), BF16), pltpu.VMEM((2, 16, 2, BS, NR), BF16),
            vmem(whole), vmem(phases[0]), vmem(joined),
            [vmem(q) for q in phases], [vmem(q) for q in phases], [vmem(q) for q in phases],
            dma((4,)), dma((2,)), dma((2, 9)), dma((2, 9)), dma((2, 6)), dma((2, 6)),
            dma((6, 2, 6)), dma((6, 2, 6)), dma((4, 3)), dma((4, 3)),
        ],
        compiler_params=pltpu.CompilerParams(
            collective_id=0, has_side_effects=True, vmem_limit_bytes=36 * 2**20
        ),
        name="main",
    )(
        par_inv[0], par_rhs[0], top_inv, jnp.swapaxes(top_rhs, 1, 2),
        pltpu.with_memory_space_constraint(acc, pltpu.VMEM), pltpu.with_memory_space_constraint(v, pltpu.VMEM),
    )
    psol, tsol = pl.pallas_call(
        tail_kernel,
        out_shape=(shape((2, BS, NR), F32), shape((2, 64, BS), F32)),
        in_specs=[vm] * 2,
        out_specs=(hb, hb),
        scratch_shapes=[dma((2,))],
        name="tail",
    )(pltpu.with_memory_space_constraint(solved, pltpu.VMEM), pltpu.with_memory_space_constraint(top, pltpu.VMEM))
    return psol[None], jnp.swapaxes(tsol, 1, 2)


def solution(mesh):
    four = P("layer", "tile", None, None)
    pair = P("layer", "tile")
    top = P("tile", None, "layer")
    in_specs = (
        four, four, four, four, top, P("tile", None, None), four, pair, pair, pair, four, pair, pair, pair,
    )
    return jax.shard_map(local, mesh=mesh, in_specs=in_specs, out_specs=(four, top), check_vma=False)
```

```python
import jax
import jax.numpy as jnp
from jax import lax
from jax.experimental import pallas as pl
from jax.experimental.pallas import tpu as pltpu
from jax.sharding import PartitionSpec as P

MESH = pl.DeviceIdType.MESH
F32, BF16 = jnp.float32, jnp.bfloat16
BS, NR = 128, 256
CH = 16
UN = 16
PARTS = (
    ((0, 1, 2), 0, 48, 0),
    ((1, 0, 2), 48, 48, 0),
    ((2, 0, 1), 96, 16, None),
    ((0, 1, 2), 0, 48, 1),
    ((1, 0, 2), 48, 48, 1),
    ((2, 1, 0), 112, 16, None),
)
LAST = ((2, 0, 48), (2, 48, 48), (1, 96, 16), (0, 112, 16))
GOES = (0, 1, 2, 0, 1, 3)


def split(t):
    hi = t.astype(BF16)
    return hi, (t - hi.astype(F32)).astype(BF16)


def rhs_cat(t):
    hi, lo = split(t)
    return jnp.concatenate([hi, hi, lo], axis=0)


def local_kernel(
    lrow, lcol, lcnt, prow, pcol, pcnt, rhs, inv, ltiles, ptiles,
    acc, vacc,
    xw, lt, pt, lsem, psem,
):
    nl, npar = lt.shape[0], pt.shape[0]
    count, pcount = lcnt[0, 0], pcnt[0, 0]

    def chunk(src, dst, sem, i):
        return pltpu.make_async_copy(src.at[pl.ds(i * CH, CH)], dst.at[pl.ds(i * CH, CH)], sem.at[i])

    for i in range(nl // CH):
        @pl.when(i * CH < count)
        def _():
            chunk(ltiles, lt, lsem, i).start()
    for i in range(npar // CH):
        @pl.when(i * CH < pcount)
        def _():
            chunk(ptiles, pt, psem, i).start()

    @pl.loop(0, acc.shape[0])
    def _(i):
        acc[i] = jnp.zeros((BS, NR), F32)

    @pl.loop(0, vacc.shape[0])
    def _(i):
        vacc[i] = jnp.zeros((2, BS, BS), F32)

    for c in range(4):
        x = jnp.dot(inv[c], rhs[c], precision=lax.Precision.HIGHEST, preferred_element_type=F32)
        xw[c] = rhs_cat(x)

    dummy, vdummy = acc.shape[0] - 1, vacc.shape[0] - 1

    def top_place(t):
        return ((t >> 1) & 1) * 32 + (t >> 2) * 2 + (t & 1)

    def group(g, _):
        @pl.when(lax.rem(g, CH // UN) == 0)
        def _():
            chunk(ltiles, lt, lsem, g // (CH // UN)).wait()

        where, prods = [], []
        for u in range(UN):
            s = g * UN + u
            r = lrow[0, s]
            par = ((r >> 1) & 1) * 8 + (r >> 4) * 2 + (r & 1)
            idx = jnp.where(r < 64, par, 16 + top_place(r - 64))
            where.append(jnp.where(s < count, idx, dummy))
            hi, lo = split(lt[s])
            w = xw[lcol[0, s]]
            prods.append(
                jnp.dot(jnp.concatenate([hi, lo], axis=1), w[:2 * BS], preferred_element_type=F32)
                + jnp.dot(hi, w[2 * BS:], preferred_element_type=F32)
            )
        for u in range(UN):
            acc[where[u]] += prods[u]
        return 0

    lax.fori_loop(0, (count + UN - 1) // UN, group, 0)
    def dense(g, _):
        @pl.when(lax.rem(g, CH // 4) == 0)
        def _():
            chunk(ptiles, pt, psem, g // (CH // 4)).wait()

        for u in range(4):
            s = g * 4 + u
            vacc[jnp.where(s < pcount, top_place(prow[0, s]), vdummy), pcol[0, s]] += pt[s]
        return 0

    lax.fori_loop(0, (pcount + 3) // 4, dense, 0)


def main_kernel(
    par_inv_in, par_rhs_in, top_inv_in, top_rhs_in, acc, v,
    x_own, tsol,
    par_inv, par_rhs, top_inv, top_rhs, total,
    g_sib, g_send, g_two, g_prev, g_next, x_sib, xw,
    l_sib, v_sib, vh, vl,
    d, e, f, two, prev, nxt,
    loc, v_sem, sib_s, sib_r, gs, gr, rs_s, rs_r, last_s, last_r,
):
    z = lax.axis_index("layer")
    tile = lax.axis_index("tile")
    x, y, c = tile // 8, (tile // 2) % 4, tile % 2
    pos = (x, y, z)

    def at(axis, step):
        q = [x, y, z]
        q[axis] = (q[axis] + step + 4) % 4
        return (q[2], q[0] * 8 + q[1] * 2 + c)

    sib = (z, x * 8 + y * 2 + 1 - c)
    barrier = pltpu.get_barrier_semaphore()
    peers = [sib] + [at(a, s) for a in range(3) for s in (1, -1, 2)]
    for p in peers:
        pl.semaphore_signal(barrier, inc=1, device_id=p, device_id_type=MESH)

    small = [
        pltpu.make_async_copy(src, dst, loc.at[i])
        for i, (src, dst) in enumerate(
            ((par_inv_in, par_inv), (par_rhs_in, par_rhs), (top_inv_in, top_inv), (top_rhs_in, top_rhs))
        )
    ]
    for copy in small:
        copy.start()

    def split_v(src, base, side):
        @pl.loop(0, 16)
        def _(k):
            for j in range(2):
                for b in range(2):
                    hi, lo = split(src[base + k * 2 + j, b])
                    vh[side, k, j, :, b * BS:(b + 1) * BS] = hi
                    vl[side, k, j, :, b * BS:(b + 1) * BS] = lo

    split_v(v, c * 32, 0)
    pl.semaphore_wait(barrier, len(peers))

    started = []

    def send(src, dst, ssem, rsem, device):
        copy = pltpu.make_async_remote_copy(
            src_ref=src, dst_ref=dst, send_sem=ssem, recv_sem=rsem, device_id=device, device_id_type=MESH
        )
        copy.start()
        started.append(copy)
        return copy

    def leave(*copies):
        for copy in copies:
            copy.wait_send()
            started[:] = [other for other in started if other is not copy]

    order = [(x + 2) % 4, (x + 1) % 4, (x + 3) % 4, x]
    yorder = [(y + 2) % 4, (y + 1) % 4, (y + 3) % 4, y]
    col = (pl.ds(0, BS), pl.ds(BS, BS))

    def swap_g(i, half):
        q = order[i]
        return send(
            acc.at[pl.ds((1 - c) * 8 + q * 2, 2), :, col[half]], g_sib.at[q, :, :, col[half]],
            sib_s.at[half, i], sib_r.at[half, i], sib,
        )

    def swap_l(i, half):
        q = order[i]
        return send(
            acc.at[pl.ds(16 + (1 - c) * 32 + q * 8, 8), :, col[half]], l_sib.at[pl.ds(q * 8, 8), :, col[half]],
            sib_s.at[half, 4 + i], sib_r.at[half, 4 + i], sib,
        )

    right, left = at(0, 1), at(0, -1)
    ring = [{}, {}]

    def gather(i, half):
        swap[half][i].wait_recv()
        q, cut = order[i], col[half]
        for j in range(2):
            g_send[i, j, :, cut] = acc[c * 8 + q * 2 + j, :, cut] + g_sib[q, j, :, cut]

    def hop(half, name, i, src, dst, device):
        cut = col[half]
        ring[half][name] = send(src.at[:, cut], dst.at[:, cut], gs.at[half, i], gr.at[half, i], device)

    def far_g(half):
        hop(half, "a2", 0, g_send.at[0, 0], g_two.at[0], right)
        hop(half, "b2", 1, g_send.at[0, 1], g_two.at[1], left)

    def near_g(half):
        hop(half, "p1", 2, g_send.at[1, 1], g_prev.at[1], right)
        hop(half, "n0", 3, g_send.at[2, 0], g_next.at[0], left)

    def relay_g(half):
        cut = col[half]
        ring[half]["a2"].wait_recv()
        g_send[1, 0, :, cut] = g_send[1, 0, :, cut] + g_two[0, :, cut]
        hop(half, "p0", 4, g_send.at[1, 0], g_prev.at[0], right)
        ring[half]["b2"].wait_recv()
        g_send[2, 1, :, cut] = g_send[2, 1, :, cut] + g_two[1, :, cut]
        hop(half, "n1", 5, g_send.at[2, 1], g_next.at[1], left)

    def solve(half):
        cut = col[half]
        for name in ("p1", "n0", "p0", "n1"):
            ring[half][name].wait_recv()
        for j in range(2):
            known = acc[c * 8 + x * 2 + j, :, cut] + g_sib[x, j, :, cut] + g_prev[j, :, cut] + g_next[j, :, cut]
            x_own[j, :, cut] = jnp.dot(
                par_inv[j], par_rhs[j, :, cut] - known, precision=lax.Precision.HIGHEST, preferred_element_type=F32
            )
        return send(
            x_own.at[:, :, col[half]], x_sib.at[:, :, col[half]], sib_s.at[half, 8], sib_r.at[half, 8], sib
        )

    def set_weights(half, side, ref):
        for j in range(2):
            hi, lo = split(ref[j, :, col[half]])
            xw[half, side, pl.ds(j * BS, BS), col[0]] = hi
            xw[half, side, pl.ds(j * BS, BS), col[1]] = lo

    swap = [[swap_g(0, 0)], [swap_g(0, 1)]]
    leave(swap[0][0], swap[1][0])
    for i in (1, 2, 3):
        for half in range(2):
            swap[half].append(swap_g(i, half))
    v_swap = send(v.at[pl.ds((1 - c) * 32, 32)], v_sib, v_sem.at[0], v_sem.at[1], sib)
    gather(0, 0)
    far_g(0)
    gather(0, 1)
    far_g(1)
    for half in range(2):
        gather(1, half)
        gather(2, half)
    leave(ring[0]["a2"], ring[0]["b2"])
    near_g(0)
    near_g(1)
    relay_g(0)
    l_swap = [[swap_l(i, 0) for i in range(4)], []]
    relay_g(1)
    v_swap.wait_recv()
    split_v(v_sib, 0, 1)
    small[0].wait()
    small[1].wait()
    for half in range(2):
        swap[half][3].wait_recv()
    x_swap = [solve(0)]
    set_weights(0, 0, x_own)
    l_swap[1] += [swap_l(i, 1) for i in range(4)]
    x_swap[0].wait_recv()
    set_weights(0, 1, x_sib)

    low = lax.broadcasted_iota(jnp.int32, (BS, BS), 1) < 64

    def products(half, spots):
        for kx, ky in spots:
            k = kx * 4 + ky
            main, fine = jnp.zeros((2 * BS, NR), F32), jnp.zeros((2 * BS, BS), F32)
            for side in range(2):
                weights = xw[half, side]
                main = main + jnp.dot(
                    vh[side, k].reshape(2 * BS, NR), weights, preferred_element_type=F32
                )
                fine = fine + jnp.dot(
                    vl[side, k].reshape(2 * BS, NR), weights[:, :BS], preferred_element_type=F32
                )
            both = main[:, :BS] + (main[:, BS:] + fine)
            sums = [
                both[j * BS:(j + 1) * BS]
                + (acc[16 + c * 32 + k * 2 + j, :, col[half]] + l_sib[k * 2 + j, :, col[half]])
                for j in range(2)
            ]
            second = pltpu.roll(sums[1], 64, 1)
            for odd in range(2):
                q = jnp.where(low, second, sums[0]) if odd else jnp.where(low, sums[0], second)
                for p, (axes, row, n, of) in enumerate(PARTS):
                    if of not in (None, half):
                        continue
                    spot = (kx, ky, odd if of is not None else half * 2 + odd)
                    s0, s1, s2 = (spot[axis] for axis in axes)
                    d[p][s0, s1, s2] = q[row:row + n]

    front, back = pl.ds(0, 2), pl.ds(2, 2)
    flying = {}

    def place(p):
        axis = PARTS[p][0][0]
        return axis, pos[axis], d[p], rs_s.at[p, 0], rs_r.at[p, 0]

    def far(p):
        axis, m, src, ss, rr = place(p)
        chunk, there = src.at[(m + 2) % 4], two[0][p]
        flying[p, "far"] = [
            send(chunk.at[front], there.at[front], ss.at[0], rr.at[0], at(axis, 1)),
            send(chunk.at[back], there.at[back], ss.at[1], rr.at[1], at(axis, -1)),
        ]

    def near(p):
        axis, m, src, ss, rr = place(p)
        flying[p, "near"] = [
            send(src.at[(m + 1) % 4, back], prev[0][p].at[back], ss.at[2], rr.at[2], at(axis, 1)),
            send(src.at[(m + 3) % 4, front], nxt[0][p].at[front], ss.at[3], rr.at[3], at(axis, -1)),
        ]

    def relay(p):
        axis, m, src, ss, rr = place(p)
        hi, lo = (m + 1) % 4, (m + 3) % 4
        ahead, behind = flying[p, "far"]
        ahead.wait_recv()
        src[hi, front] = src[hi, front] + two[0][p][front]
        one = send(src.at[hi, front], prev[0][p].at[front], ss.at[4], rr.at[4], at(axis, 1))
        behind.wait_recv()
        src[lo, back] = src[lo, back] + two[0][p][back]
        other = send(src.at[lo, back], nxt[0][p].at[back], ss.at[5], rr.at[5], at(axis, -1))
        flying[p, "relay"] = [one, other]

    def straight(key, axis, src, ph, i, ss, rr):
        m = pos[axis]
        flying[key] = [
            send(src.at[(m + step) % 4], there[ph][i], ss.at[k], rr.at[k], at(axis, step))
            for k, (step, there) in enumerate(((2, two), (1, prev), (3, nxt)))
        ]

    def received(key, axis, src, ph, i):
        for copy in flying[key]:
            copy.wait_recv()
        return src[pos[axis]] + prev[ph][i][...] + nxt[ph][i][...] + two[ph][i][...]

    def second_phase(p):
        axis, m, src, ss, rr = place(p)
        for copy in flying[p, "near"] + flying[p, "relay"]:
            copy.wait_recv()
        e[p][...] = src[m] + prev[0][p][...] + nxt[0][p][...]
        straight((p, 1), PARTS[p][0][1], e[p], 1, p, rs_s.at[p, 1], rs_r.at[p, 1])

    def join(p):
        got = received((p, 1), PARTS[p][0][1], e[p], 1, p)
        of = PARTS[p][3]
        if of is None:
            f[GOES[p]][...] = got
        else:
            f[GOES[p]][pl.ds(2 * of, 2)] = got

    def third_phase(i):
        straight((i, 2), LAST[i][0], f[i], 2, i, last_s.at[i], last_r.at[i])

    l_swap[0][0].wait_recv()
    products(0, [(order[0], q) for q in yorder])
    far(0)
    for i in (1, 2, 3):
        l_swap[0][i].wait_recv()
    products(0, [(q, yorder[0]) for q in order[1:]])
    far(1)
    x_swap.append(solve(1))
    products(0, [(q, k) for q in order[1:] for k in yorder[1:]])
    near(0)
    near(1)
    set_weights(1, 0, x_own)
    x_swap[1].wait_recv()
    set_weights(1, 1, x_sib)
    l_swap[1][0].wait_recv()
    products(1, [(order[0], q) for q in yorder])
    far(3)
    for i in (1, 2, 3):
        l_swap[1][i].wait_recv()
    products(1, [(q, yorder[0]) for q in order[1:]])
    far(4)
    relay(0)
    relay(1)
    products(1, [(q, k) for q in order[1:] for k in yorder[1:]])
    far(2)
    far(5)
    near(3)
    near(4)
    near(2)
    relay(3)
    relay(4)
    relay(2)
    near(5)
    second_phase(0)
    second_phase(1)
    relay(5)
    for p in (3, 4, 2, 5):
        second_phase(p)
    join(0)
    join(1)
    join(3)
    third_phase(0)
    join(4)
    third_phase(1)
    join(2)
    third_phase(2)
    join(5)
    third_phase(3)
    for i, (axis, row, n) in enumerate(LAST):
        total[pl.ds(row, n)] = received((i, 2), axis, f[i], 2, i)

    turned = jnp.where(z % 2 == 1, pltpu.roll(total[...], 64, 1), total[...]).T
    small[2].wait()
    small[3].wait()
    for j in range(2):
        tsol[j] = lax.dot_general(
            top_rhs[j] - turned[j * 64:(j + 1) * 64], top_inv[j], (((1,), (1,)), ((), ())),
            precision=lax.Precision.HIGHEST, preferred_element_type=F32,
        )
    for copy in started:
        copy.wait_send()


def tail_kernel(solved, top, psol, tsol, sem):
    copies = (pltpu.make_async_copy(solved, psol, sem.at[0]), pltpu.make_async_copy(top, tsol, sem.at[1]))
    for copy in copies:
        copy.start()
    for copy in copies:
        copy.wait()


def leaf_call(*args):
    vm = pl.BlockSpec(memory_space=pltpu.VMEM)
    sm = pl.BlockSpec(memory_space=pltpu.SMEM)
    hb = pl.BlockSpec(memory_space=pl.ANY)
    nl, npar = args[8].shape[0], args[9].shape[0]
    shape = jax.ShapeDtypeStruct
    return pl.pallas_call(
        local_kernel,
        out_shape=(
            pltpu.VMEM((81, BS, NR), F32),
            pltpu.VMEM((65, 2, BS, BS), F32),
        ),
        in_specs=[sm] * 6 + [vm, vm, hb, hb],
        out_specs=(vm, vm),
        scratch_shapes=[
            pltpu.VMEM((4, 3 * BS, NR), BF16),
            pltpu.VMEM((nl, BS, BS), F32),
            pltpu.VMEM((npar, BS, BS), F32),
            pltpu.SemaphoreType.DMA((nl // CH,)),
            pltpu.SemaphoreType.DMA((npar // CH,)),
        ],
        compiler_params=pltpu.CompilerParams(vmem_limit_bytes=36*2**20),
        name="leaf",
    )(*args)


def local(
    leaf_rhs, leaf_inv, par_rhs, par_inv, top_rhs, top_inv, leaf_tiles, leaf_cols, leaf_rows, leaf_count,
    par_tiles, par_cols, par_rows, par_count,
):
    vm = pl.BlockSpec(memory_space=pltpu.VMEM)
    shape = jax.ShapeDtypeStruct
    acc, v = leaf_call(
        leaf_rows, leaf_cols, leaf_count, par_rows, par_cols, par_count,
        leaf_rhs[0], leaf_inv[0], leaf_tiles[0], par_tiles[0],
    )
    dma = pltpu.SemaphoreType.DMA
    hb = pl.BlockSpec(memory_space=pl.ANY)
    whole = [(4, 4, 4 if of is None else 2, n, BS) for _, _, n, of in PARTS]
    joined = [(4, n, BS) for _, _, n in LAST]
    phases = [[q[1:] for q in whole], [q[2:] for q in whole], [q[1:] for q in joined]]

    def vmem(shapes):
        return [pltpu.VMEM(q, F32) for q in shapes]

    block, square, slim = pltpu.VMEM((2, BS, NR), F32), pltpu.VMEM((2, BS, BS), F32), pltpu.VMEM((2, 64, BS), F32)
    solved, top = pl.pallas_call(
        main_kernel,
        out_shape=(block, slim),
        in_specs=[hb] * 4 + [vm] * 2,
        out_specs=(vm, vm),
        scratch_shapes=[
            square, block, square, slim, pltpu.VMEM((BS, BS), F32),
            pltpu.VMEM((4, 2, BS, NR), F32), pltpu.VMEM((3, 2, BS, NR), F32), block, block, block,
            block, pltpu.VMEM((2, 2, 2 * BS, 2 * BS), BF16),
            pltpu.VMEM((32, BS, NR), F32), pltpu.VMEM((32, 2, BS, BS), F32),
            pltpu.VMEM((2, 16, 2, BS, NR), BF16), pltpu.VMEM((2, 16, 2, BS, NR), BF16),
            vmem(whole), vmem(phases[0]), vmem(joined),
            [vmem(q) for q in phases], [vmem(q) for q in phases], [vmem(q) for q in phases],
            dma((4,)), dma((2,)), dma((2, 9)), dma((2, 9)), dma((2, 6)), dma((2, 6)),
            dma((6, 2, 6)), dma((6, 2, 6)), dma((4, 3)), dma((4, 3)),
        ],
        compiler_params=pltpu.CompilerParams(
            collective_id=0, has_side_effects=True, vmem_limit_bytes=36 * 2**20
        ),
        name="main",
    )(
        par_inv[0], par_rhs[0], top_inv, jnp.swapaxes(top_rhs, 1, 2),
        pltpu.with_memory_space_constraint(acc, pltpu.VMEM), pltpu.with_memory_space_constraint(v, pltpu.VMEM),
    )
    psol, tsol = pl.pallas_call(
        tail_kernel,
        out_shape=(shape((2, BS, NR), F32), shape((2, 64, BS), F32)),
        in_specs=[vm] * 2,
        out_specs=(hb, hb),
        scratch_shapes=[dma((2,))],
        name="tail",
    )(pltpu.with_memory_space_constraint(solved, pltpu.VMEM), pltpu.with_memory_space_constraint(top, pltpu.VMEM))
    return psol[None], jnp.swapaxes(tsol, 1, 2)


def solution(mesh):
    four = P("layer", "tile", None, None)
    pair = P("layer", "tile")
    top = P("tile", None, "layer")
    in_specs = (
        four, four, four, four, top, P("tile", None, None), four, pair, pair, pair, four, pair, pair, pair,
    )
    return jax.shard_map(local, mesh=mesh, in_specs=in_specs, out_specs=(four, top), check_vma=False)
```

```python
import jax
import jax.numpy as jnp
from jax import lax
from jax.experimental import pallas as pl
from jax.experimental.pallas import tpu as pltpu
from jax.sharding import PartitionSpec as P

MESH = pl.DeviceIdType.MESH
F32, BF16 = jnp.float32, jnp.bfloat16
BS, NR = 128, 256
CH = 16
UN = 32
PARTS = (
    ((0, 1, 2), 0, 48, 0),
    ((1, 0, 2), 48, 48, 0),
    ((2, 0, 1), 96, 16, None),
    ((0, 1, 2), 0, 48, 1),
    ((1, 0, 2), 48, 48, 1),
    ((2, 1, 0), 112, 16, None),
)
LAST = ((2, 0, 48), (2, 48, 48), (1, 96, 16), (0, 112, 16))
GOES = (0, 1, 2, 0, 1, 3)


def split(t):
    hi = t.astype(BF16)
    return hi, (t - hi.astype(F32)).astype(BF16)


def rhs_cat(t):
    hi, lo = split(t)
    return jnp.concatenate([hi, hi, lo], axis=0)


def local_kernel(
    lrow, lcol, lcnt, prow, pcol, pcnt, rhs, inv, ltiles, ptiles,
    acc, vacc,
    xw, lt, pt, lsem, psem,
):
    nl, npar = lt.shape[0], pt.shape[0]
    count, pcount = lcnt[0, 0], pcnt[0, 0]

    def chunk(src, dst, sem, i):
        return pltpu.make_async_copy(src.at[pl.ds(i * CH, CH)], dst.at[pl.ds(i * CH, CH)], sem.at[i])

    for i in range(nl // CH):
        @pl.when(i * CH < count)
        def _():
            chunk(ltiles, lt, lsem, i).start()
    for i in range(npar // CH):
        @pl.when(i * CH < pcount)
        def _():
            chunk(ptiles, pt, psem, i).start()

    @pl.loop(0, acc.shape[0])
    def _(i):
        acc[i] = jnp.zeros((BS, NR), F32)

    @pl.loop(0, vacc.shape[0])
    def _(i):
        vacc[i] = jnp.zeros((2, BS, BS), F32)

    for c in range(4):
        x = jnp.dot(inv[c], rhs[c], precision=lax.Precision.HIGHEST, preferred_element_type=F32)
        xw[c] = rhs_cat(x)

    dummy, vdummy = acc.shape[0] - 1, vacc.shape[0] - 1

    def top_place(t):
        return ((t >> 1) & 1) * 32 + (t >> 2) * 2 + (t & 1)

    def group(g, _):
        for i in range(UN // CH):
            @pl.when((g * (UN // CH) + i) * CH < count)
            def _():
                chunk(ltiles, lt, lsem, g * (UN // CH) + i).wait()

        where, prods = [], []
        for u in range(UN):
            s = g * UN + u
            r = lrow[0, s]
            par = ((r >> 1) & 1) * 8 + (r >> 4) * 2 + (r & 1)
            idx = jnp.where(r < 64, par, 16 + top_place(r - 64))
            where.append(jnp.where(s < count, idx, dummy))
            hi, lo = split(lt[s])
            w = xw[lcol[0, s]]
            prods.append(
                jnp.dot(jnp.concatenate([hi, lo], axis=1), w[:2 * BS], preferred_element_type=F32)
                + jnp.dot(hi, w[2 * BS:], preferred_element_type=F32)
            )
        for u in range(UN):
            acc[where[u]] += prods[u]
        return 0

    lax.fori_loop(0, (count + UN - 1) // UN, group, 0)
    def dense(g, _):
        @pl.when(lax.rem(g, CH // 4) == 0)
        def _():
            chunk(ptiles, pt, psem, g // (CH // 4)).wait()

        for u in range(4):
            s = g * 4 + u
            vacc[jnp.where(s < pcount, top_place(prow[0, s]), vdummy), pcol[0, s]] += pt[s]
        return 0

    lax.fori_loop(0, (pcount + 3) // 4, dense, 0)


def main_kernel(
    par_inv_in, par_rhs_in, top_inv_in, top_rhs_in, acc, v,
    x_own, tsol,
    par_inv, par_rhs, top_inv, top_rhs, total,
    g_sib, g_send, g_two, g_prev, g_next, x_sib, xw,
    l_sib, v_sib, vh, vl,
    d, e, f, two, prev, nxt,
    loc, v_sem, sib_s, sib_r, gs, gr, rs_s, rs_r, last_s, last_r,
):
    z = lax.axis_index("layer")
    tile = lax.axis_index("tile")
    x, y, c = tile // 8, (tile // 2) % 4, tile % 2
    pos = (x, y, z)

    def at(axis, step):
        q = [x, y, z]
        q[axis] = (q[axis] + step + 4) % 4
        return (q[2], q[0] * 8 + q[1] * 2 + c)

    sib = (z, x * 8 + y * 2 + 1 - c)
    barrier = pltpu.get_barrier_semaphore()
    peers = [sib] + [at(a, s) for a in range(3) for s in (1, -1, 2)]
    for p in peers:
        pl.semaphore_signal(barrier, inc=1, device_id=p, device_id_type=MESH)

    small = [
        pltpu.make_async_copy(src, dst, loc.at[i])
        for i, (src, dst) in enumerate(
            ((par_inv_in, par_inv), (par_rhs_in, par_rhs), (top_inv_in, top_inv), (top_rhs_in, top_rhs))
        )
    ]
    for copy in small:
        copy.start()

    def split_v(src, base, side):
        @pl.loop(0, 16)
        def _(k):
            for j in range(2):
                for b in range(2):
                    hi, lo = split(src[base + k * 2 + j, b])
                    vh[side, k, j, :, b * BS:(b + 1) * BS] = hi
                    vl[side, k, j, :, b * BS:(b + 1) * BS] = lo

    split_v(v, c * 32, 0)
    pl.semaphore_wait(barrier, len(peers))

    started = []

    def send(src, dst, ssem, rsem, device):
        copy = pltpu.make_async_remote_copy(
            src_ref=src, dst_ref=dst, send_sem=ssem, recv_sem=rsem, device_id=device, device_id_type=MESH
        )
        copy.start()
        started.append(copy)
        return copy

    def leave(*copies):
        for copy in copies:
            copy.wait_send()
            started[:] = [other for other in started if other is not copy]

    order = [(x + 2) % 4, (x + 1) % 4, (x + 3) % 4, x]
    yorder = [(y + 2) % 4, (y + 1) % 4, (y + 3) % 4, y]
    col = (pl.ds(0, BS), pl.ds(BS, BS))

    def swap_g(i, half):
        q = order[i]
        return send(
            acc.at[pl.ds((1 - c) * 8 + q * 2, 2), :, col[half]], g_sib.at[q, :, :, col[half]],
            sib_s.at[half, i], sib_r.at[half, i], sib,
        )

    def swap_l(i, half):
        q = order[i]
        return send(
            acc.at[pl.ds(16 + (1 - c) * 32 + q * 8, 8), :, col[half]], l_sib.at[pl.ds(q * 8, 8), :, col[half]],
            sib_s.at[half, 4 + i], sib_r.at[half, 4 + i], sib,
        )

    right, left = at(0, 1), at(0, -1)
    ring = [{}, {}]

    def gather(i, half):
        swap[half][i].wait_recv()
        q, cut = order[i], col[half]
        for j in range(2):
            g_send[i, j, :, cut] = acc[c * 8 + q * 2 + j, :, cut] + g_sib[q, j, :, cut]

    def hop(half, name, i, src, dst, device):
        cut = col[half]
        ring[half][name] = send(src.at[:, cut], dst.at[:, cut], gs.at[half, i], gr.at[half, i], device)

    def far_g(half):
        hop(half, "a2", 0, g_send.at[0, 0], g_two.at[0], right)
        hop(half, "b2", 1, g_send.at[0, 1], g_two.at[1], left)

    def near_g(half):
        hop(half, "p1", 2, g_send.at[1, 1], g_prev.at[1], right)
        hop(half, "n0", 3, g_send.at[2, 0], g_next.at[0], left)

    def relay_g(half):
        cut = col[half]
        ring[half]["a2"].wait_recv()
        g_send[1, 0, :, cut] = g_send[1, 0, :, cut] + g_two[0, :, cut]
        hop(half, "p0", 4, g_send.at[1, 0], g_prev.at[0], right)
        ring[half]["b2"].wait_recv()
        g_send[2, 1, :, cut] = g_send[2, 1, :, cut] + g_two[1, :, cut]
        hop(half, "n1", 5, g_send.at[2, 1], g_next.at[1], left)

    def solve(half):
        cut = col[half]
        for name in ("p1", "n0", "p0", "n1"):
            ring[half][name].wait_recv()
        for j in range(2):
            known = acc[c * 8 + x * 2 + j, :, cut] + g_sib[x, j, :, cut] + g_prev[j, :, cut] + g_next[j, :, cut]
            x_own[j, :, cut] = jnp.dot(
                par_inv[j], par_rhs[j, :, cut] - known, precision=lax.Precision.HIGHEST, preferred_element_type=F32
            )
        return send(
            x_own.at[:, :, col[half]], x_sib.at[:, :, col[half]], sib_s.at[half, 8], sib_r.at[half, 8], sib
        )

    def set_weights(half, side, ref):
        for j in range(2):
            hi, lo = split(ref[j, :, col[half]])
            xw[half, side, pl.ds(j * BS, BS), col[0]] = hi
            xw[half, side, pl.ds(j * BS, BS), col[1]] = lo

    swap = [[swap_g(0, 0)], [swap_g(0, 1)]]
    leave(swap[0][0], swap[1][0])
    for i in (1, 2, 3):
        for half in range(2):
            swap[half].append(swap_g(i, half))
    v_swap = send(v.at[pl.ds((1 - c) * 32, 32)], v_sib, v_sem.at[0], v_sem.at[1], sib)
    gather(0, 0)
    far_g(0)
    gather(0, 1)
    far_g(1)
    for half in range(2):
        gather(1, half)
        gather(2, half)
    leave(ring[0]["a2"], ring[0]["b2"])
    near_g(0)
    near_g(1)
    relay_g(0)
    l_swap = [[swap_l(i, 0) for i in range(4)], []]
    relay_g(1)
    v_swap.wait_recv()
    split_v(v_sib, 0, 1)
    small[0].wait()
    small[1].wait()
    for half in range(2):
        swap[half][3].wait_recv()
    x_swap = [solve(0)]
    set_weights(0, 0, x_own)
    l_swap[1] += [swap_l(i, 1) for i in range(4)]
    x_swap[0].wait_recv()
    set_weights(0, 1, x_sib)

    low = lax.broadcasted_iota(jnp.int32, (BS, BS), 1) < 64

    def products(half, spots):
        for kx, ky in spots:
            k = kx * 4 + ky
            main, fine = jnp.zeros((2 * BS, NR), F32), jnp.zeros((2 * BS, BS), F32)
            for side in range(2):
                weights = xw[half, side]
                main = main + jnp.dot(
                    vh[side, k].reshape(2 * BS, NR), weights, preferred_element_type=F32
                )
                fine = fine + jnp.dot(
                    vl[side, k].reshape(2 * BS, NR), weights[:, :BS], preferred_element_type=F32
                )
            both = main[:, :BS] + (main[:, BS:] + fine)
            sums = [
                both[j * BS:(j + 1) * BS]
                + (acc[16 + c * 32 + k * 2 + j, :, col[half]] + l_sib[k * 2 + j, :, col[half]])
                for j in range(2)
            ]
            second = pltpu.roll(sums[1], 64, 1)
            for odd in range(2):
                q = jnp.where(low, second, sums[0]) if odd else jnp.where(low, sums[0], second)
                for p, (axes, row, n, of) in enumerate(PARTS):
                    if of not in (None, half):
                        continue
                    spot = (kx, ky, odd if of is not None else half * 2 + odd)
                    s0, s1, s2 = (spot[axis] for axis in axes)
                    d[p][s0, s1, s2] = q[row:row + n]

    front, back = pl.ds(0, 2), pl.ds(2, 2)
    flying = {}

    def place(p):
        axis = PARTS[p][0][0]
        return axis, pos[axis], d[p], rs_s.at[p, 0], rs_r.at[p, 0]

    def far(p):
        axis, m, src, ss, rr = place(p)
        chunk, there = src.at[(m + 2) % 4], two[0][p]
        flying[p, "far"] = [
            send(chunk.at[front], there.at[front], ss.at[0], rr.at[0], at(axis, 1)),
            send(chunk.at[back], there.at[back], ss.at[1], rr.at[1], at(axis, -1)),
        ]

    def near(p):
        axis, m, src, ss, rr = place(p)
        flying[p, "near"] = [
            send(src.at[(m + 1) % 4, back], prev[0][p].at[back], ss.at[2], rr.at[2], at(axis, 1)),
            send(src.at[(m + 3) % 4, front], nxt[0][p].at[front], ss.at[3], rr.at[3], at(axis, -1)),
        ]

    def relay(p):
        axis, m, src, ss, rr = place(p)
        hi, lo = (m + 1) % 4, (m + 3) % 4
        ahead, behind = flying[p, "far"]
        ahead.wait_recv()
        src[hi, front] = src[hi, front] + two[0][p][front]
        one = send(src.at[hi, front], prev[0][p].at[front], ss.at[4], rr.at[4], at(axis, 1))
        behind.wait_recv()
        src[lo, back] = src[lo, back] + two[0][p][back]
        other = send(src.at[lo, back], nxt[0][p].at[back], ss.at[5], rr.at[5], at(axis, -1))
        flying[p, "relay"] = [one, other]

    def straight(key, axis, src, ph, i, ss, rr):
        m = pos[axis]
        flying[key] = [
            send(src.at[(m + step) % 4], there[ph][i], ss.at[k], rr.at[k], at(axis, step))
            for k, (step, there) in enumerate(((2, two), (1, prev), (3, nxt)))
        ]

    def received(key, axis, src, ph, i):
        for copy in flying[key]:
            copy.wait_recv()
        return src[pos[axis]] + prev[ph][i][...] + nxt[ph][i][...] + two[ph][i][...]

    def second_phase(p):
        axis, m, src, ss, rr = place(p)
        for copy in flying[p, "near"] + flying[p, "relay"]:
            copy.wait_recv()
        e[p][...] = src[m] + prev[0][p][...] + nxt[0][p][...]
        straight((p, 1), PARTS[p][0][1], e[p], 1, p, rs_s.at[p, 1], rs_r.at[p, 1])

    def join(p):
        got = received((p, 1), PARTS[p][0][1], e[p], 1, p)
        of = PARTS[p][3]
        if of is None:
            f[GOES[p]][...] = got
        else:
            f[GOES[p]][pl.ds(2 * of, 2)] = got

    def third_phase(i):
        straight((i, 2), LAST[i][0], f[i], 2, i, last_s.at[i], last_r.at[i])

    l_swap[0][0].wait_recv()
    products(0, [(order[0], q) for q in yorder])
    far(0)
    for i in (1, 2, 3):
        l_swap[0][i].wait_recv()
    products(0, [(q, yorder[0]) for q in order[1:]])
    far(1)
    x_swap.append(solve(1))
    products(0, [(q, k) for q in order[1:] for k in yorder[1:]])
    near(0)
    near(1)
    set_weights(1, 0, x_own)
    x_swap[1].wait_recv()
    set_weights(1, 1, x_sib)
    l_swap[1][0].wait_recv()
    products(1, [(order[0], q) for q in yorder])
    far(3)
    for i in (1, 2, 3):
        l_swap[1][i].wait_recv()
    products(1, [(q, yorder[0]) for q in order[1:]])
    far(4)
    relay(0)
    relay(1)
    products(1, [(q, k) for q in order[1:] for k in yorder[1:]])
    far(2)
    far(5)
    near(3)
    near(4)
    near(2)
    relay(3)
    relay(4)
    relay(2)
    near(5)
    second_phase(0)
    second_phase(1)
    relay(5)
    for p in (3, 4, 2, 5):
        second_phase(p)
    join(0)
    join(1)
    join(3)
    third_phase(0)
    join(4)
    third_phase(1)
    join(2)
    third_phase(2)
    join(5)
    third_phase(3)
    for i, (axis, row, n) in enumerate(LAST):
        total[pl.ds(row, n)] = received((i, 2), axis, f[i], 2, i)

    turned = jnp.where(z % 2 == 1, pltpu.roll(total[...], 64, 1), total[...]).T
    small[2].wait()
    small[3].wait()
    for j in range(2):
        tsol[j] = lax.dot_general(
            top_rhs[j] - turned[j * 64:(j + 1) * 64], top_inv[j], (((1,), (1,)), ((), ())),
            precision=lax.Precision.HIGHEST, preferred_element_type=F32,
        )
    for copy in started:
        copy.wait_send()


def tail_kernel(solved, top, psol, tsol, sem):
    copies = (pltpu.make_async_copy(solved, psol, sem.at[0]), pltpu.make_async_copy(top, tsol, sem.at[1]))
    for copy in copies:
        copy.start()
    for copy in copies:
        copy.wait()


def leaf_call(*args):
    vm = pl.BlockSpec(memory_space=pltpu.VMEM)
    sm = pl.BlockSpec(memory_space=pltpu.SMEM)
    hb = pl.BlockSpec(memory_space=pl.ANY)
    nl, npar = args[8].shape[0], args[9].shape[0]
    shape = jax.ShapeDtypeStruct
    return pl.pallas_call(
        local_kernel,
        out_shape=(
            pltpu.VMEM((81, BS, NR), F32),
            pltpu.VMEM((65, 2, BS, BS), F32),
        ),
        in_specs=[sm] * 6 + [vm, vm, hb, hb],
        out_specs=(vm, vm),
        scratch_shapes=[
            pltpu.VMEM((4, 3 * BS, NR), BF16),
            pltpu.VMEM((nl, BS, BS), F32),
            pltpu.VMEM((npar, BS, BS), F32),
            pltpu.SemaphoreType.DMA((nl // CH,)),
            pltpu.SemaphoreType.DMA((npar // CH,)),
        ],
        compiler_params=pltpu.CompilerParams(vmem_limit_bytes=36*2**20),
        name="leaf",
    )(*args)


def local(
    leaf_rhs, leaf_inv, par_rhs, par_inv, top_rhs, top_inv, leaf_tiles, leaf_cols, leaf_rows, leaf_count,
    par_tiles, par_cols, par_rows, par_count,
):
    vm = pl.BlockSpec(memory_space=pltpu.VMEM)
    shape = jax.ShapeDtypeStruct
    acc, v = leaf_call(
        leaf_rows, leaf_cols, leaf_count, par_rows, par_cols, par_count,
        leaf_rhs[0], leaf_inv[0], leaf_tiles[0], par_tiles[0],
    )
    dma = pltpu.SemaphoreType.DMA
    hb = pl.BlockSpec(memory_space=pl.ANY)
    whole = [(4, 4, 4 if of is None else 2, n, BS) for _, _, n, of in PARTS]
    joined = [(4, n, BS) for _, _, n in LAST]
    phases = [[q[1:] for q in whole], [q[2:] for q in whole], [q[1:] for q in joined]]

    def vmem(shapes):
        return [pltpu.VMEM(q, F32) for q in shapes]

    block, square, slim = pltpu.VMEM((2, BS, NR), F32), pltpu.VMEM((2, BS, BS), F32), pltpu.VMEM((2, 64, BS), F32)
    solved, top = pl.pallas_call(
        main_kernel,
        out_shape=(block, slim),
        in_specs=[hb] * 4 + [vm] * 2,
        out_specs=(vm, vm),
        scratch_shapes=[
            square, block, square, slim, pltpu.VMEM((BS, BS), F32),
            pltpu.VMEM((4, 2, BS, NR), F32), pltpu.VMEM((3, 2, BS, NR), F32), block, block, block,
            block, pltpu.VMEM((2, 2, 2 * BS, 2 * BS), BF16),
            pltpu.VMEM((32, BS, NR), F32), pltpu.VMEM((32, 2, BS, BS), F32),
            pltpu.VMEM((2, 16, 2, BS, NR), BF16), pltpu.VMEM((2, 16, 2, BS, NR), BF16),
            vmem(whole), vmem(phases[0]), vmem(joined),
            [vmem(q) for q in phases], [vmem(q) for q in phases], [vmem(q) for q in phases],
            dma((4,)), dma((2,)), dma((2, 9)), dma((2, 9)), dma((2, 6)), dma((2, 6)),
            dma((6, 2, 6)), dma((6, 2, 6)), dma((4, 3)), dma((4, 3)),
        ],
        compiler_params=pltpu.CompilerParams(
            collective_id=0, has_side_effects=True, vmem_limit_bytes=36 * 2**20
        ),
        name="main",
    )(
        par_inv[0], par_rhs[0], top_inv, jnp.swapaxes(top_rhs, 1, 2),
        pltpu.with_memory_space_constraint(acc, pltpu.VMEM), pltpu.with_memory_space_constraint(v, pltpu.VMEM),
    )
    psol, tsol = pl.pallas_call(
        tail_kernel,
        out_shape=(shape((2, BS, NR), F32), shape((2, 64, BS), F32)),
        in_specs=[vm] * 2,
        out_specs=(hb, hb),
        scratch_shapes=[dma((2,))],
        name="tail",
    )(pltpu.with_memory_space_constraint(solved, pltpu.VMEM), pltpu.with_memory_space_constraint(top, pltpu.VMEM))
    return psol[None], jnp.swapaxes(tsol, 1, 2)


def solution(mesh):
    four = P("layer", "tile", None, None)
    pair = P("layer", "tile")
    top = P("tile", None, "layer")
    in_specs = (
        four, four, four, four, top, P("tile", None, None), four, pair, pair, pair, four, pair, pair, pair,
    )
    return jax.shard_map(local, mesh=mesh, in_specs=in_specs, out_specs=(four, top), check_vma=False)
```

```python
import jax
import jax.numpy as jnp
from jax import lax
from jax.experimental import pallas as pl
from jax.experimental.pallas import tpu as pltpu
from jax.sharding import PartitionSpec as P

MESH = pl.DeviceIdType.MESH
F32, BF16 = jnp.float32, jnp.bfloat16
BS, NR = 128, 256
CH = 16
UN = 32
PARTS = (
    ((0, 1, 2), 0, 48, 0),
    ((1, 0, 2), 48, 48, 0),
    ((2, 0, 1), 96, 16, None),
    ((0, 1, 2), 0, 48, 1),
    ((1, 0, 2), 48, 48, 1),
    ((2, 1, 0), 112, 16, None),
)
LAST = ((2, 0, 48), (2, 48, 48), (1, 96, 16), (0, 112, 16))
GOES = (0, 1, 2, 0, 1, 3)


def split(t):
    hi = t.astype(BF16)
    return hi, (t - hi.astype(F32)).astype(BF16)


def rhs_cat(t):
    hi, lo = split(t)
    return jnp.concatenate([hi, hi, lo], axis=0)


def local_kernel(
    lrow, lcol, lcnt, prow, pcol, pcnt, rhs, inv, ltiles, ptiles,
    acc, vacc,
    xw, lt, pt, lsem, psem,
):
    nl, npar = lt.shape[0], pt.shape[0]
    count, pcount = lcnt[0, 0], pcnt[0, 0]

    def chunk(src, dst, sem, i):
        return pltpu.make_async_copy(src.at[pl.ds(i * CH, CH)], dst.at[pl.ds(i * CH, CH)], sem.at[i])

    for i in range(nl // CH):
        @pl.when(i * CH < count)
        def _():
            chunk(ltiles, lt, lsem, i).start()
    for i in range(npar // CH):
        @pl.when(i * CH < pcount)
        def _():
            chunk(ptiles, pt, psem, i).start()

    @pl.loop(0, acc.shape[0])
    def _(i):
        acc[i] = jnp.zeros((BS, NR), F32)

    @pl.loop(0, vacc.shape[0])
    def _(i):
        vacc[i] = jnp.zeros((2, BS, BS), F32)

    for c in range(4):
        x = jnp.dot(inv[c], rhs[c], precision=lax.Precision.HIGHEST, preferred_element_type=F32)
        xw[c] = rhs_cat(x)

    dummy, vdummy = acc.shape[0] - 1, vacc.shape[0] - 1

    def top_place(t):
        return ((t >> 1) & 1) * 32 + (t >> 2) * 2 + (t & 1)

    def group(g, _):
        for i in range(UN // CH):
            @pl.when((g * (UN // CH) + i) * CH < count)
            def _():
                chunk(ltiles, lt, lsem, g * (UN // CH) + i).wait()

        where, prods = [], []
        for u in range(UN):
            s = g * UN + u
            r = lrow[0, s]
            par = ((r >> 1) & 1) * 8 + (r >> 4) * 2 + (r & 1)
            idx = jnp.where(r < 64, par, 16 + top_place(r - 64))
            where.append(jnp.where(s < count, idx, dummy))
            hi, lo = split(lt[s])
            w = xw[lcol[0, s]]
            prods.append(
                jnp.dot(jnp.concatenate([hi, lo], axis=1), w[:2 * BS], preferred_element_type=F32)
                + jnp.dot(hi, w[2 * BS:], preferred_element_type=F32)
            )
        for u in range(UN):
            acc[where[u]] += prods[u]
        return 0

    lax.fori_loop(0, (count + UN - 1) // UN, group, 0)
    def dense(g, _):
        @pl.when(lax.rem(g, CH // 4) == 0)
        def _():
            chunk(ptiles, pt, psem, g // (CH // 4)).wait()

        for u in range(4):
            s = g * 4 + u
            vacc[jnp.where(s < pcount, top_place(prow[0, s]), vdummy), pcol[0, s]] += pt[s]
        return 0

    lax.fori_loop(0, (pcount + 3) // 4, dense, 0)


def main_kernel(
    par_inv_in, par_rhs_in, top_inv_in, top_rhs_in, acc, v,
    x_own, tsol,
    par_inv, par_rhs, top_inv, top_rhs, total,
    g_sib, g_send, g_two, g_prev, g_next, x_sib, xw,
    l_sib, v_sib, vh, vl,
    d, e, f, two, prev, nxt,
    loc, v_sem, sib_s, sib_r, gs, gr, rs_s, rs_r, last_s, last_r,
):
    z = lax.axis_index("layer")
    tile = lax.axis_index("tile")
    x, y, c = tile // 8, (tile // 2) % 4, tile % 2
    pos = (x, y, z)

    def at(axis, step):
        q = [x, y, z]
        q[axis] = (q[axis] + step + 4) % 4
        return (q[2], q[0] * 8 + q[1] * 2 + c)

    sib = (z, x * 8 + y * 2 + 1 - c)
    barrier = pltpu.get_barrier_semaphore()
    peers = [sib] + [at(a, s) for a in range(3) for s in (1, -1, 2)]
    for p in peers:
        pl.semaphore_signal(barrier, inc=1, device_id=p, device_id_type=MESH)

    small = [
        pltpu.make_async_copy(src, dst, loc.at[i])
        for i, (src, dst) in enumerate(
            ((par_inv_in, par_inv), (par_rhs_in, par_rhs), (top_inv_in, top_inv), (top_rhs_in, top_rhs))
        )
    ]
    for copy in small:
        copy.start()

    def split_v(src, base, side):
        @pl.loop(0, 16)
        def _(k):
            for j in range(2):
                for b in range(2):
                    hi, lo = split(src[base + k * 2 + j, b])
                    vh[side, k, j, :, b * BS:(b + 1) * BS] = hi
                    vl[side, k, j, :, b * BS:(b + 1) * BS] = lo

    split_v(v, c * 32, 0)
    pl.semaphore_wait(barrier, len(peers))

    started = []

    def send(src, dst, ssem, rsem, device):
        copy = pltpu.make_async_remote_copy(
            src_ref=src, dst_ref=dst, send_sem=ssem, recv_sem=rsem, device_id=device, device_id_type=MESH
        )
        copy.start()
        started.append(copy)
        return copy

    def leave(*copies):
        for copy in copies:
            copy.wait_send()
            started[:] = [other for other in started if other is not copy]

    order = [(x + 2) % 4, (x + 1) % 4, (x + 3) % 4, x]
    yorder = [(y + 2) % 4, (y + 1) % 4, (y + 3) % 4, y]
    col = (pl.ds(0, BS), pl.ds(BS, BS))

    def swap_g(i, half):
        q = order[i]
        return send(
            acc.at[pl.ds((1 - c) * 8 + q * 2, 2), :, col[half]], g_sib.at[q, :, :, col[half]],
            sib_s.at[half, i], sib_r.at[half, i], sib,
        )

    def swap_l(i, half):
        q = order[i]
        return send(
            acc.at[pl.ds(16 + (1 - c) * 32 + q * 8, 8), :, col[half]], l_sib.at[pl.ds(q * 8, 8), :, col[half]],
            sib_s.at[half, 4 + i], sib_r.at[half, 4 + i], sib,
        )

    right, left = at(0, 1), at(0, -1)
    ring = [{}, {}]

    def gather(i, half):
        swap[half][i].wait_recv()
        q, cut = order[i], col[half]
        for j in range(2):
            g_send[i, j, :, cut] = acc[c * 8 + q * 2 + j, :, cut] + g_sib[q, j, :, cut]

    def hop(half, name, i, src, dst, device):
        cut = col[half]
        ring[half][name] = send(src.at[:, cut], dst.at[:, cut], gs.at[half, i], gr.at[half, i], device)

    def far_g(half):
        hop(half, "a2", 0, g_send.at[0, 0], g_two.at[0], right)
        hop(half, "b2", 1, g_send.at[0, 1], g_two.at[1], left)

    def near_g(half):
        hop(half, "p1", 2, g_send.at[1, 1], g_prev.at[1], right)
        hop(half, "n0", 3, g_send.at[2, 0], g_next.at[0], left)

    def relay_g(half):
        cut = col[half]
        ring[half]["a2"].wait_recv()
        g_send[1, 0, :, cut] = g_send[1, 0, :, cut] + g_two[0, :, cut]
        hop(half, "p0", 4, g_send.at[1, 0], g_prev.at[0], right)
        ring[half]["b2"].wait_recv()
        g_send[2, 1, :, cut] = g_send[2, 1, :, cut] + g_two[1, :, cut]
        hop(half, "n1", 5, g_send.at[2, 1], g_next.at[1], left)

    def solve(half):
        cut = col[half]
        for name in ("p1", "n0", "p0", "n1"):
            ring[half][name].wait_recv()
        for j in range(2):
            known = acc[c * 8 + x * 2 + j, :, cut] + g_sib[x, j, :, cut] + g_prev[j, :, cut] + g_next[j, :, cut]
            x_own[j, :, cut] = jnp.dot(
                par_inv[j], par_rhs[j, :, cut] - known, precision=lax.Precision.HIGHEST, preferred_element_type=F32
            )
        return send(
            x_own.at[:, :, col[half]], x_sib.at[:, :, col[half]], sib_s.at[half, 8], sib_r.at[half, 8], sib
        )

    def set_weights(half, side, ref):
        for j in range(2):
            hi, lo = split(ref[j, :, col[half]])
            xw[half, side, pl.ds(j * BS, BS), col[0]] = hi
            xw[half, side, pl.ds(j * BS, BS), col[1]] = lo

    swap = [[swap_g(0, 0)], [swap_g(0, 1)]]
    leave(swap[0][0], swap[1][0])
    for i in (1, 2, 3):
        for half in range(2):
            swap[half].append(swap_g(i, half))
    v_swap = send(v.at[pl.ds((1 - c) * 32, 32)], v_sib, v_sem.at[0], v_sem.at[1], sib)
    gather(0, 0)
    far_g(0)
    gather(0, 1)
    far_g(1)
    for half in range(2):
        gather(1, half)
        gather(2, half)
    leave(ring[0]["a2"], ring[0]["b2"])
    near_g(0)
    near_g(1)
    relay_g(0)
    l_swap = [[swap_l(i, 0) for i in range(4)], []]
    relay_g(1)
    v_swap.wait_recv()
    split_v(v_sib, 0, 1)
    small[0].wait()
    small[1].wait()
    for half in range(2):
        swap[half][3].wait_recv()
    x_swap = [solve(0)]
    set_weights(0, 0, x_own)
    l_swap[1] += [swap_l(i, 1) for i in range(4)]
    x_swap[0].wait_recv()
    set_weights(0, 1, x_sib)

    low = lax.broadcasted_iota(jnp.int32, (BS, BS), 1) < 64

    def products(half, spots):
        for kx, ky in spots:
            k = kx * 4 + ky
            main, fine = jnp.zeros((2 * BS, NR), F32), jnp.zeros((2 * BS, BS), F32)
            for side in range(2):
                weights = xw[half, side]
                main = main + jnp.dot(
                    vh[side, k].reshape(2 * BS, NR), weights, preferred_element_type=F32
                )
                fine = fine + jnp.dot(
                    vl[side, k].reshape(2 * BS, NR), weights[:, :BS], preferred_element_type=F32
                )
            both = main[:, :BS] + (main[:, BS:] + fine)
            sums = [
                both[j * BS:(j + 1) * BS]
                + (acc[16 + c * 32 + k * 2 + j, :, col[half]] + l_sib[k * 2 + j, :, col[half]])
                for j in range(2)
            ]
            second = pltpu.roll(sums[1], 64, 1)
            for odd in range(2):
                q = jnp.where(low, second, sums[0]) if odd else jnp.where(low, sums[0], second)
                for p, (axes, row, n, of) in enumerate(PARTS):
                    if of not in (None, half):
                        continue
                    spot = (kx, ky, odd if of is not None else half * 2 + odd)
                    s0, s1, s2 = (spot[axis] for axis in axes)
                    d[p][s0, s1, s2] = q[row:row + n]

    front, back = pl.ds(0, 2), pl.ds(2, 2)
    flying = {}

    def place(p):
        axis = PARTS[p][0][0]
        return axis, pos[axis], d[p], rs_s.at[p, 0], rs_r.at[p, 0]

    def far(p):
        axis, m, src, ss, rr = place(p)
        chunk, there = src.at[(m + 2) % 4], two[0][p]
        flying[p, "far"] = [
            send(chunk.at[front], there.at[front], ss.at[0], rr.at[0], at(axis, 1)),
            send(chunk.at[back], there.at[back], ss.at[1], rr.at[1], at(axis, -1)),
        ]

    def near(p):
        axis, m, src, ss, rr = place(p)
        flying[p, "near"] = [
            send(src.at[(m + 1) % 4, back], prev[0][p].at[back], ss.at[2], rr.at[2], at(axis, 1)),
            send(src.at[(m + 3) % 4, front], nxt[0][p].at[front], ss.at[3], rr.at[3], at(axis, -1)),
        ]

    def relay(p):
        axis, m, src, ss, rr = place(p)
        hi, lo = (m + 1) % 4, (m + 3) % 4
        ahead, behind = flying[p, "far"]
        ahead.wait_recv()
        src[hi, front] = src[hi, front] + two[0][p][front]
        one = send(src.at[hi, front], prev[0][p].at[front], ss.at[4], rr.at[4], at(axis, 1))
        behind.wait_recv()
        src[lo, back] = src[lo, back] + two[0][p][back]
        other = send(src.at[lo, back], nxt[0][p].at[back], ss.at[5], rr.at[5], at(axis, -1))
        flying[p, "relay"] = [one, other]

    def straight(key, axis, src, ph, i, ss, rr):
        m = pos[axis]
        flying[key] = [
            send(src.at[(m + step) % 4], there[ph][i], ss.at[k], rr.at[k], at(axis, step))
            for k, (step, there) in enumerate(((2, two), (1, prev), (3, nxt)))
        ]

    def received(key, axis, src, ph, i):
        for copy in flying[key]:
            copy.wait_recv()
        return src[pos[axis]] + prev[ph][i][...] + nxt[ph][i][...] + two[ph][i][...]

    def second_phase(p):
        axis, m, src, ss, rr = place(p)
        for copy in flying[p, "near"] + flying[p, "relay"]:
            copy.wait_recv()
        e[p][...] = src[m] + prev[0][p][...] + nxt[0][p][...]
        straight((p, 1), PARTS[p][0][1], e[p], 1, p, rs_s.at[p, 1], rs_r.at[p, 1])

    def join(p):
        got = received((p, 1), PARTS[p][0][1], e[p], 1, p)
        of = PARTS[p][3]
        if of is None:
            f[GOES[p]][...] = got
        else:
            f[GOES[p]][pl.ds(2 * of, 2)] = got

    def third_phase(i):
        straight((i, 2), LAST[i][0], f[i], 2, i, last_s.at[i], last_r.at[i])

    l_swap[0][0].wait_recv()
    products(0, [(order[0], q) for q in yorder])
    far(0)
    for i in (1, 2, 3):
        l_swap[0][i].wait_recv()
    products(0, [(q, yorder[0]) for q in order[1:]])
    far(1)
    x_swap.append(solve(1))
    products(0, [(q, k) for q in order[1:3] for k in yorder[1:]])
    near(0)
    products(0, [(order[3], k) for k in yorder[1:3]])
    near(1)
    products(0, [(order[3], yorder[3])])
    set_weights(1, 0, x_own)
    x_swap[1].wait_recv()
    set_weights(1, 1, x_sib)
    l_swap[1][0].wait_recv()
    products(1, [(order[0], q) for q in yorder])
    far(3)
    for i in (1, 2, 3):
        l_swap[1][i].wait_recv()
    products(1, [(q, yorder[0]) for q in order[1:]])
    far(4)
    relay(0)
    relay(1)
    products(1, [(q, k) for q in order[1:] for k in yorder[1:]])
    far(2)
    far(5)
    near(3)
    near(4)
    near(2)
    relay(3)
    relay(4)
    relay(2)
    near(5)
    second_phase(0)
    second_phase(1)
    relay(5)
    for p in (3, 4, 2, 5):
        second_phase(p)
    join(0)
    join(1)
    join(3)
    third_phase(0)
    join(4)
    third_phase(1)
    join(2)
    third_phase(2)
    join(5)
    third_phase(3)
    for i, (axis, row, n) in enumerate(LAST):
        total[pl.ds(row, n)] = received((i, 2), axis, f[i], 2, i)

    turned = jnp.where(z % 2 == 1, pltpu.roll(total[...], 64, 1), total[...]).T
    small[2].wait()
    small[3].wait()
    for j in range(2):
        tsol[j] = lax.dot_general(
            top_rhs[j] - turned[j * 64:(j + 1) * 64], top_inv[j], (((1,), (1,)), ((), ())),
            precision=lax.Precision.HIGHEST, preferred_element_type=F32,
        )
    for copy in started:
        copy.wait_send()


def tail_kernel(solved, top, psol, tsol, sem):
    copies = (pltpu.make_async_copy(solved, psol, sem.at[0]), pltpu.make_async_copy(top, tsol, sem.at[1]))
    for copy in copies:
        copy.start()
    for copy in copies:
        copy.wait()


def leaf_call(*args):
    vm = pl.BlockSpec(memory_space=pltpu.VMEM)
    sm = pl.BlockSpec(memory_space=pltpu.SMEM)
    hb = pl.BlockSpec(memory_space=pl.ANY)
    nl, npar = args[8].shape[0], args[9].shape[0]
    shape = jax.ShapeDtypeStruct
    return pl.pallas_call(
        local_kernel,
        out_shape=(
            pltpu.VMEM((81, BS, NR), F32),
            pltpu.VMEM((65, 2, BS, BS), F32),
        ),
        in_specs=[sm] * 6 + [vm, vm, hb, hb],
        out_specs=(vm, vm),
        scratch_shapes=[
            pltpu.VMEM((4, 3 * BS, NR), BF16),
            pltpu.VMEM((nl, BS, BS), F32),
            pltpu.VMEM((npar, BS, BS), F32),
            pltpu.SemaphoreType.DMA((nl // CH,)),
            pltpu.SemaphoreType.DMA((npar // CH,)),
        ],
        compiler_params=pltpu.CompilerParams(vmem_limit_bytes=36*2**20),
        name="leaf",
    )(*args)


def local(
    leaf_rhs, leaf_inv, par_rhs, par_inv, top_rhs, top_inv, leaf_tiles, leaf_cols, leaf_rows, leaf_count,
    par_tiles, par_cols, par_rows, par_count,
):
    vm = pl.BlockSpec(memory_space=pltpu.VMEM)
    shape = jax.ShapeDtypeStruct
    acc, v = leaf_call(
        leaf_rows, leaf_cols, leaf_count, par_rows, par_cols, par_count,
        leaf_rhs[0], leaf_inv[0], leaf_tiles[0], par_tiles[0],
    )
    dma = pltpu.SemaphoreType.DMA
    hb = pl.BlockSpec(memory_space=pl.ANY)
    whole = [(4, 4, 4 if of is None else 2, n, BS) for _, _, n, of in PARTS]
    joined = [(4, n, BS) for _, _, n in LAST]
    phases = [[q[1:] for q in whole], [q[2:] for q in whole], [q[1:] for q in joined]]

    def vmem(shapes):
        return [pltpu.VMEM(q, F32) for q in shapes]

    block, square, slim = pltpu.VMEM((2, BS, NR), F32), pltpu.VMEM((2, BS, BS), F32), pltpu.VMEM((2, 64, BS), F32)
    solved, top = pl.pallas_call(
        main_kernel,
        out_shape=(block, slim),
        in_specs=[hb] * 4 + [vm] * 2,
        out_specs=(vm, vm),
        scratch_shapes=[
            square, block, square, slim, pltpu.VMEM((BS, BS), F32),
            pltpu.VMEM((4, 2, BS, NR), F32), pltpu.VMEM((3, 2, BS, NR), F32), block, block, block,
            block, pltpu.VMEM((2, 2, 2 * BS, 2 * BS), BF16),
            pltpu.VMEM((32, BS, NR), F32), pltpu.VMEM((32, 2, BS, BS), F32),
            pltpu.VMEM((2, 16, 2, BS, NR), BF16), pltpu.VMEM((2, 16, 2, BS, NR), BF16),
            vmem(whole), vmem(phases[0]), vmem(joined),
            [vmem(q) for q in phases], [vmem(q) for q in phases], [vmem(q) for q in phases],
            dma((4,)), dma((2,)), dma((2, 9)), dma((2, 9)), dma((2, 6)), dma((2, 6)),
            dma((6, 2, 6)), dma((6, 2, 6)), dma((4, 3)), dma((4, 3)),
        ],
        compiler_params=pltpu.CompilerParams(
            collective_id=0, has_side_effects=True, vmem_limit_bytes=36 * 2**20
        ),
        name="main",
    )(
        par_inv[0], par_rhs[0], top_inv, jnp.swapaxes(top_rhs, 1, 2),
        pltpu.with_memory_space_constraint(acc, pltpu.VMEM), pltpu.with_memory_space_constraint(v, pltpu.VMEM),
    )
    psol, tsol = pl.pallas_call(
        tail_kernel,
        out_shape=(shape((2, BS, NR), F32), shape((2, 64, BS), F32)),
        in_specs=[vm] * 2,
        out_specs=(hb, hb),
        scratch_shapes=[dma((2,))],
        name="tail",
    )(pltpu.with_memory_space_constraint(solved, pltpu.VMEM), pltpu.with_memory_space_constraint(top, pltpu.VMEM))
    return psol[None], jnp.swapaxes(tsol, 1, 2)


def solution(mesh):
    four = P("layer", "tile", None, None)
    pair = P("layer", "tile")
    top = P("tile", None, "layer")
    in_specs = (
        four, four, four, four, top, P("tile", None, None), four, pair, pair, pair, four, pair, pair, pair,
    )
    return jax.shard_map(local, mesh=mesh, in_specs=in_specs, out_specs=(four, top), check_vma=False)
```
